512 devices in a mesh: rows: 2 (over y_lo), hidden: 8 (over y_hi, x), latents: 32 (over z, core).
Axes of the slice: x: 4, y: 4 (y_hi: 2, y_lo: 2; y = y_hi * 2 + y_lo), z: 16, core: 2. Of those that a mesh axis runs over, the one named last changes fastest.
Arguments:
- inputs: bfloat16 [256, 3584], P('rows', ('hidden', 'latents')), may hold values from -6 to 6
- gate_weight: bfloat16 [3584, 14336], P(None, ('hidden', 'latents')), may hold values from -0.09375 to 0.09375
- up_weight: bfloat16 [3584, 14336], P(None, ('hidden', 'latents')), may hold values from -0.09375 to 0.09375
- down_weight: bfloat16 [14336, 3584], P(('hidden', 'latents')), may hold values from -0.046875 to 0.046875
- encoder: bfloat16 [3584, 65536], P('hidden', ('rows', 'latents')), may hold values from -0.09375 to 0.09375
- decoder: bfloat16 [65536, 3584], P(('rows', 'latents'), 'hidden'), may hold values from -0.09375 to 0.09375
- enc_bias: float32 [65536], P(('rows', 'latents')), may hold values from -3 to 3
- dec_bias: float32 [3584], P('hidden'), may hold values from -3 to 3
- shuffle_order: int32 [256], replicated, may hold values from 0 to 255, each once
Outputs:
- recon_out: bfloat16 [256, 3584], P(('rows', 'latents'), 'hidden')
- grad_enc: bfloat16 [3584, 65536], P('hidden', ('rows', 'latents'))
- grad_dec: bfloat16 [65536, 3584], P(('rows', 'latents'), 'hidden')
The draws below stay inside these ranges and needn't reach their ends.
Inputs may be any that keep to these rules, and one draw needn't show every extreme that they name: shuffle_order names every token index 0 to 255 exactly once.
All inputs are finite; a program needn't handle non-finite values.
Results may differ from the reference program's by a relative error of at most 0.038.
Values may be sent and summed in bfloat16 or wider, within the bound.
No kernel may reach another device: no remote copies, remote signals or barrier semaphores. Data moves between devices by JAX's collectives and lax.ppermute only.
A program may use at most 64 MiB of HBM per device.

```python
import math
import jax
import jax.numpy as jnp
from jax import lax

D = 3584
FF = 14336
LATENTS = 65536
TOKENS = 256
N_HIDDEN = 8


def steps_of(stream_key, dims, cuts, least, largest):
    loudness, own = 1.0, jax.random.fold_in(stream_key, 6)
    for position, shards_of in cuts:
        heights = jnp.exp(jax.random.uniform(jax.random.fold_in(own, position), (shards_of,), jnp.float32, least / len(cuts), largest / len(cuts)))
        loudness = loudness * jnp.repeat(heights, dims[position] // shards_of).reshape([-1 if axis == position else 1 for axis in range(len(dims))])
    return loudness


def gaussian(rng, shape, scale, bound, cuts=(), dtype=jnp.bfloat16):
    gain = steps_of(rng, shape, cuts, -0.22, 0.18) if cuts else 1.0
    result = jax.random.normal(rng, shape, jnp.float32) * scale * gain
    return jnp.minimum(jnp.maximum(result, -bound), bound).astype(dtype)


def setup_inputs(seed: int = 0) -> dict:
    key_list = jax.random.split(jax.random.key(seed), 10)
    return {
        "inputs": gaussian(key_list[0], (TOKENS, D), 1.0, 6.0, ((0, 2), (1, 256))),
        "gate_weight": gaussian(key_list[1], (D, FF), D ** -0.5, 0.09375, ((1, 256),)),
        "up_weight": gaussian(key_list[2], (D, FF), D ** -0.5, 0.09375, ((1, 256),)),
        "down_weight": gaussian(key_list[3], (FF, D), FF ** -0.5, 0.046875, ((0, 256),)),
        "encoder": gaussian(key_list[4], (D, LATENTS), D ** -0.5, 0.09375, ((0, 8), (1, 64))),
        "decoder": gaussian(key_list[5], (LATENTS, D), D ** -0.5, 0.09375, ((0, 64), (1, 8))),
        "enc_bias": gaussian(key_list[6], (LATENTS,), 0.5, 3.0, ((0, 64),), jnp.float32),
        "dec_bias": gaussian(key_list[7], (D,), 0.5, 3.0, ((0, 8),), jnp.float32),
        "shuffle_order": jax.random.permutation(key_list[8], TOKENS).astype(jnp.int32),
    }


smooth_scale = 0.1
sparsity_weight = 0.5

def blockwise(left, right_rows):
    width = D // N_HIDDEN
    total = None
    for shard in range(N_HIDDEN):
        piece = jnp.dot(left[:, shard * width:(shard + 1) * width], right_rows[shard * width:(shard + 1) * width, :], preferred_element_type=jnp.float32)
        piece = lax.optimization_barrier(piece.astype(jnp.bfloat16)).astype(jnp.float32)
        total = piece if total is None else total + piece
    return total

def reference(inputs, gate_weight, up_weight, down_weight, encoder, decoder, enc_bias, dec_bias, shuffle_order):
    gate_act = jnp.dot(inputs, gate_weight, preferred_element_type=jnp.float32)
    up_act = jnp.dot(inputs, up_weight, preferred_element_type=jnp.float32)
    hidden = (jax.nn.gelu(gate_act, approximate=True) * up_act).astype(jnp.bfloat16)
    mlp_out = jnp.dot(hidden, down_weight, preferred_element_type=jnp.float32).astype(jnp.bfloat16)
    shuffled = jnp.take(mlp_out, shuffle_order.astype(jnp.int32), axis=0)
    pre_act = blockwise(shuffled, encoder) + enc_bias[None, :]
    latent_act = (smooth_scale * jax.nn.softplus(pre_act / smooth_scale)).astype(jnp.bfloat16)
    recon = jnp.dot(latent_act, decoder, preferred_element_type=jnp.float32) + dec_bias[None, :]
    recon_out = recon.astype(jnp.bfloat16)
    scale = 1.0 / math.sqrt(TOKENS)
    d_err = (scale * (recon - shuffled.astype(jnp.float32))).astype(jnp.bfloat16)
    grad_dec = jnp.dot(latent_act.T, d_err, preferred_element_type=jnp.float32).astype(jnp.bfloat16)
    d_latent = blockwise(d_err, decoder.T)
    d_pre = ((d_latent + sparsity_weight * scale) * jax.nn.sigmoid(pre_act / smooth_scale)).astype(jnp.bfloat16)
    grad_enc = jnp.dot(shuffled.T, d_pre, preferred_element_type=jnp.float32).astype(jnp.bfloat16)
    return (recon_out, grad_enc, grad_dec)
```

```python
import math

import jax
import jax.numpy as jnp
from jax import lax
from jax.sharding import Mesh
from jax.sharding import PartitionSpec as P

R, Y, X, Z, C = "rows", "hidden_0", "hidden_1", "latents_0", "latents_1"
HIDDEN = (Y, X)
LATENTS = (Z, C)
HIDDEN_LATENTS = (Y, X, Z, C)
ROWS_LATENTS = (R, Z, C)
ROWS_Z = (R, Z)

smooth_scale = 0.1
sparsity_weight = 0.5
F32 = jnp.float32
BF16 = jnp.bfloat16


def exchange(blocks, axes):
    return lax.all_to_all(blocks, axes, 0, 0, tiled=True)


def sent_to_all(x, axes):
    return exchange(jnp.broadcast_to(x, (lax.axis_size(axes), *x.shape)), axes)


def both_cores(x):
    return lax.all_gather(x, C, axis=0, tiled=False)


def total(blocks):
    return jnp.sum(blocks.astype(F32), axis=0)


def own(x, index, dim):
    return lax.dynamic_index_in_dim(x, index, dim, keepdims=False)


def shards(
    inputs, gate_weight, up_weight, down_weight, encoder, decoder, enc_bias, dec_bias, shuffle_order
):
    tokens = shuffle_order.shape[0]
    n_hidden = lax.axis_size(HIDDEN)
    n_z = lax.axis_size(Z)
    n_rows_z = lax.axis_size(ROWS_Z)
    core = lax.axis_index(C)
    width = decoder.shape[1]
    half = width // 2
    latents = encoder.shape[1]
    units = gate_weight.shape[1]

    few = sent_to_all(inputs.T, Z)
    more = sent_to_all(few, HIDDEN)
    every = both_cores(more)
    gathered = every.transpose(1, 2, 0, 3, 4).reshape(-1, inputs.shape[0])
    both_weights = jnp.concatenate([gate_weight, up_weight], axis=1)
    acts = lax.dot_general(
        both_weights, gathered, (((0,), (0,)), ((), ())), preferred_element_type=F32
    )
    hidden = (jax.nn.gelu(acts[:units], approximate=True) * acts[units:]).astype(BF16)
    part = lax.dot_general(
        down_weight, hidden, (((0,), (0,)), ((), ())), preferred_element_type=F32
    ).astype(BF16)

    pair = total(both_cores(part)).reshape(n_hidden, 2, half, -1)
    mine = own(pair, core, 1).astype(BF16)
    summed = total(exchange(mine, HIDDEN)).T.astype(BF16)
    rows_own = total(exchange(summed.reshape(n_z, -1, half), Z)).astype(BF16)
    mlp_out = both_cores(sent_to_all(rows_own, ROWS_Z).reshape(tokens, half))

    order = shuffle_order.reshape(n_rows_z, 2, -1).transpose(1, 0, 2).reshape(-1)
    pick = (order[:, None] == jnp.arange(tokens)[None, :]).astype(BF16)
    shuffled = jnp.concatenate(
        [jnp.dot(pick, mlp_out[c], preferred_element_type=F32).astype(BF16) for c in range(2)],
        axis=1,
    )
    pre_local = jnp.dot(shuffled, encoder, preferred_element_type=F32).astype(BF16)
    pre_act = total(exchange(pre_local.reshape(n_hidden, -1, latents), HIDDEN)) + enc_bias[None, :]
    latent_own = (smooth_scale * jax.nn.softplus(pre_act / smooth_scale)).astype(BF16)
    latent_act = sent_to_all(latent_own, HIDDEN).reshape(tokens, latents)
    recon_local = jnp.dot(latent_act, decoder, preferred_element_type=F32)
    recon_pair = jnp.sum(both_cores(recon_local), axis=0)
    recon_mine = own(recon_pair.reshape(2, n_rows_z, -1, width), core, 0).astype(BF16)
    recon = total(exchange(recon_mine, ROWS_Z)) + dec_bias[None, :]
    recon_out = recon.astype(BF16)

    scale = 1.0 / math.sqrt(tokens)
    count = recon.shape[0]
    first = (core * n_rows_z + lax.axis_index(ROWS_Z)) * count
    target = lax.dynamic_slice_in_dim(shuffled, first, count, 0)
    err_own = (scale * (recon - target.astype(F32))).astype(BF16)
    d_err = both_cores(sent_to_all(err_own, ROWS_Z).reshape(-1, width)).reshape(tokens, width)

    back_local = lax.dot_general(
        d_err, decoder, (((1,), (1,)), ((), ())), preferred_element_type=F32
    ).astype(BF16)
    d_latent = total(exchange(back_local.reshape(n_hidden, -1, latents), HIDDEN))
    grad_dec = lax.dot_general(
        latent_act, d_err, (((0,), (0,)), ((), ())), preferred_element_type=F32
    ).astype(BF16)
    d_pre_own = (
        (d_latent + sparsity_weight * scale) * jax.nn.sigmoid(pre_act / smooth_scale)
    ).astype(BF16)
    d_pre = sent_to_all(d_pre_own, HIDDEN).reshape(tokens, latents)
    grad_enc = lax.dot_general(
        shuffled, d_pre, (((0,), (0,)), ((), ())), preferred_element_type=F32
    ).astype(BF16)
    return (recon_out, grad_enc, grad_dec)


def solution(mesh):
    finer = Mesh(
        mesh.devices.reshape(mesh.shape["rows"], 2, 4, 16, 2),
        (R, Y, X, Z, C),
    )
    return jax.shard_map(
        shards,
        mesh=finer,
        in_specs=(
            P(R, HIDDEN_LATENTS),
            P(None, HIDDEN_LATENTS),
            P(None, HIDDEN_LATENTS),
            P(HIDDEN_LATENTS, None),
            P(HIDDEN, ROWS_LATENTS),
            P(ROWS_LATENTS, HIDDEN),
            P(ROWS_LATENTS),
            P(HIDDEN),
            P(),
        ),
        out_specs=(P(ROWS_LATENTS, HIDDEN), P(HIDDEN, ROWS_LATENTS), P(ROWS_LATENTS, HIDDEN)),
        check_vma=False,
    )
```

```python
import math

import jax
import jax.numpy as jnp
from jax import lax
from jax.sharding import Mesh
from jax.sharding import PartitionSpec as P

R, Y, X, Z, C = "rows", "hidden_0", "hidden_1", "latents_0", "latents_1"
HIDDEN = (Y, X)
LATENTS = (Z, C)
HIDDEN_LATENTS = (Y, X, Z, C)
ROWS_LATENTS = (R, Z, C)
ROWS_Z = (R, Z)

smooth_scale = 0.1
sparsity_weight = 0.5
F32 = jnp.float32
BF16 = jnp.bfloat16


def exchange(blocks, axes):
    return lax.all_to_all(blocks, axes, 0, 0, tiled=True)


def sent_to_all(x, axes):
    return exchange(jnp.broadcast_to(x, (lax.axis_size(axes), *x.shape)), axes)


def both_cores(x):
    return lax.all_gather(x, C, axis=0, tiled=False)


def swapped(x):
    return lax.ppermute(x, C, [(0, 1), (1, 0)])


def total(blocks):
    return jnp.sum(blocks.astype(F32), axis=0)


def own(x, index, dim):
    return lax.dynamic_index_in_dim(x, index, dim, keepdims=False)


def shards(
    inputs, gate_weight, up_weight, down_weight, encoder, decoder, enc_bias, dec_bias, shuffle_order
):
    tokens = shuffle_order.shape[0]
    n_hidden = lax.axis_size(HIDDEN)
    n_z = lax.axis_size(Z)
    n_rows_z = lax.axis_size(ROWS_Z)
    core = lax.axis_index(C)
    width = decoder.shape[1]
    half = width // 2
    latents = encoder.shape[1]
    units = gate_weight.shape[1]

    blocks = down_weight.reshape(units, n_hidden, 2, half)
    kept, given = own(blocks, core, 2), own(blocks, 1 - core, 2)
    taken = swapped(given)
    down_pair = jnp.concatenate(
        [jnp.where(core == 0, kept, taken), jnp.where(core == 0, taken, kept)]
    ).reshape(2 * units, n_hidden * half)

    few = sent_to_all(inputs.T, Z)
    more = sent_to_all(few, HIDDEN)
    every = both_cores(more)
    gathered = every.transpose(1, 2, 0, 3, 4).reshape(-1, inputs.shape[0])
    both_weights = jnp.concatenate([gate_weight, up_weight], axis=1)
    acts = lax.dot_general(
        both_weights, gathered, (((0,), (0,)), ((), ())), preferred_element_type=F32
    )
    hidden = (jax.nn.gelu(acts[:units], approximate=True) * acts[units:]).astype(BF16)
    hidden_pair = both_cores(hidden).reshape(2 * units, -1)
    mine = lax.dot_general(
        down_pair, hidden_pair, (((0,), (0,)), ((), ())), preferred_element_type=F32
    ).astype(BF16).reshape(n_hidden, half, -1)

    summed = total(exchange(mine, HIDDEN)).T.astype(BF16)
    rows_own = total(exchange(summed.reshape(n_z, -1, half), Z)).astype(BF16)
    mlp_out = both_cores(sent_to_all(rows_own, ROWS_Z).reshape(tokens, half))

    order = shuffle_order.reshape(n_rows_z, 2, -1).transpose(1, 0, 2).reshape(-1)
    pick = (order[:, None] == jnp.arange(tokens)[None, :]).astype(BF16)
    shuffled = jnp.concatenate(
        [jnp.dot(pick, mlp_out[c], preferred_element_type=F32).astype(BF16) for c in range(2)],
        axis=1,
    )
    pre_local = jnp.dot(shuffled, encoder, preferred_element_type=F32).astype(BF16)
    pre_act = total(exchange(pre_local.reshape(n_hidden, -1, latents), HIDDEN)) + enc_bias[None, :]
    latent_own = (smooth_scale * jax.nn.softplus(pre_act / smooth_scale)).astype(BF16)
    latent_act = sent_to_all(latent_own, HIDDEN).reshape(tokens, latents)
    halves = latent_act.reshape(2, -1, latents)
    recon_other = jnp.dot(own(halves, 1 - core, 0), decoder, preferred_element_type=F32)
    recon_own = jnp.dot(own(halves, core, 0), decoder, preferred_element_type=F32)
    recon_mine = (recon_own + swapped(recon_other)).astype(BF16).reshape(n_rows_z, -1, width)
    recon = total(exchange(recon_mine, ROWS_Z)) + dec_bias[None, :]
    recon_out = recon.astype(BF16)

    scale = 1.0 / math.sqrt(tokens)
    count = recon.shape[0]
    first = (core * n_rows_z + lax.axis_index(ROWS_Z)) * count
    target = lax.dynamic_slice_in_dim(shuffled, first, count, 0)
    err_own = (scale * (recon - target.astype(F32))).astype(BF16)
    d_err = both_cores(sent_to_all(err_own, ROWS_Z).reshape(-1, width)).reshape(tokens, width)

    back_local = lax.dot_general(
        d_err, decoder, (((1,), (1,)), ((), ())), preferred_element_type=F32
    ).astype(BF16)
    d_latent = total(exchange(back_local.reshape(n_hidden, -1, latents), HIDDEN))
    grad_dec = lax.dot_general(
        latent_act, d_err, (((0,), (0,)), ((), ())), preferred_element_type=F32
    ).astype(BF16)
    d_pre_own = (
        (d_latent + sparsity_weight * scale) * jax.nn.sigmoid(pre_act / smooth_scale)
    ).astype(BF16)
    d_pre = sent_to_all(d_pre_own, HIDDEN).reshape(tokens, latents)
    grad_enc = lax.dot_general(
        shuffled, d_pre, (((0,), (0,)), ((), ())), preferred_element_type=F32
    ).astype(BF16)
    return (recon_out, grad_enc, grad_dec)


def solution(mesh):
    finer = Mesh(
        mesh.devices.reshape(mesh.shape["rows"], 2, 4, 16, 2),
        (R, Y, X, Z, C),
    )
    return jax.shard_map(
        shards,
        mesh=finer,
        in_specs=(
            P(R, HIDDEN_LATENTS),
            P(None, HIDDEN_LATENTS),
            P(None, HIDDEN_LATENTS),
            P(HIDDEN_LATENTS, None),
            P(HIDDEN, ROWS_LATENTS),
            P(ROWS_LATENTS, HIDDEN),
            P(ROWS_LATENTS),
            P(HIDDEN),
            P(),
        ),
        out_specs=(P(ROWS_LATENTS, HIDDEN), P(HIDDEN, ROWS_LATENTS), P(ROWS_LATENTS, HIDDEN)),
        check_vma=False,
    )
```

```python
import math

import jax
import jax.numpy as jnp
from jax import lax
from jax.sharding import Mesh
from jax.sharding import PartitionSpec as P

R, Y, X, Z, C = "rows", "hidden_0", "hidden_1", "latents_0", "latents_1"
HIDDEN = (Y, X)
LATENTS = (Z, C)
HIDDEN_LATENTS = (Y, X, Z, C)
ROWS_LATENTS = (R, Z, C)
ROWS_Z = (R, Z)

smooth_scale = 0.1
sparsity_weight = 0.5
F32 = jnp.float32
BF16 = jnp.bfloat16


def exchange(blocks, axes):
    return lax.all_to_all(blocks, axes, 0, 0, tiled=True)


def sent_to_all(x, axes):
    return exchange(jnp.broadcast_to(x, (lax.axis_size(axes), *x.shape)), axes)


def both_cores(x):
    return lax.all_gather(x, C, axis=0, tiled=False)


def swapped(x):
    return lax.ppermute(x, C, [(0, 1), (1, 0)])


def total(blocks):
    return jnp.sum(blocks.astype(F32), axis=0)


def own(x, index, dim):
    return lax.dynamic_index_in_dim(x, index, dim, keepdims=False)


def shards(
    inputs, gate_weight, up_weight, down_weight, encoder, decoder, enc_bias, dec_bias, shuffle_order
):
    tokens = shuffle_order.shape[0]
    n_hidden = lax.axis_size(HIDDEN)
    n_z = lax.axis_size(Z)
    n_rows_z = lax.axis_size(ROWS_Z)
    core = lax.axis_index(C)
    width = decoder.shape[1]
    half = width // 2
    latents = encoder.shape[1]
    units = gate_weight.shape[1]

    weights = lax.optimization_barrier(jnp.concatenate([gate_weight.T, up_weight.T], axis=0))
    few = sent_to_all(inputs.T, Z)

    few, down = lax.optimization_barrier((few, down_weight))
    blocks = down.reshape(units, n_hidden, 2, half)
    kept, given = own(blocks, core, 2), own(blocks, 1 - core, 2)
    taken = swapped(given)
    down_pair = jnp.concatenate(
        [jnp.where(core == 0, kept, taken), jnp.where(core == 0, taken, kept)]
    ).reshape(2 * units, n_hidden * half)

    every = both_cores(sent_to_all(few, HIDDEN))
    gathered = every.transpose(1, 2, 0, 3, 4).reshape(-1, inputs.shape[0])
    acts = jnp.dot(weights, gathered, preferred_element_type=F32)
    hidden = (jax.nn.gelu(acts[:units], approximate=True) * acts[units:]).astype(BF16)
    hidden_pair = both_cores(hidden).reshape(2 * units, -1)
    mine = lax.dot_general(
        down_pair, hidden_pair, (((0,), (0,)), ((), ())), preferred_element_type=F32
    ).astype(BF16).reshape(n_hidden, half, -1)

    summed = total(exchange(mine, HIDDEN)).T.astype(BF16)
    rows_own = total(exchange(summed.reshape(n_z, -1, half), Z)).astype(BF16)
    mlp_out = both_cores(sent_to_all(rows_own, ROWS_Z).reshape(tokens, half))

    pick = (shuffle_order[:, None] == jnp.arange(tokens)[None, :]).astype(BF16)
    shuffled = jnp.concatenate(
        [jnp.dot(pick, mlp_out[c], preferred_element_type=F32).astype(BF16) for c in range(2)],
        axis=1,
    )
    shuffled_t = lax.optimization_barrier(shuffled.T)
    pre_local = jnp.dot(shuffled, encoder, preferred_element_type=F32).astype(BF16)
    pre_act = total(exchange(pre_local.reshape(n_hidden, -1, latents), HIDDEN)) + enc_bias[None, :]
    latent_own = (smooth_scale * jax.nn.softplus(pre_act / smooth_scale)).astype(BF16)
    latent_act = sent_to_all(latent_own, HIDDEN).reshape(tokens, latents)
    recon_local = lax.dot_general(
        decoder, latent_act, (((0,), (1,)), ((), ())), preferred_element_type=F32
    ).astype(BF16)
    recon_pair = both_cores(recon_local).reshape(2, 2, half, tokens)
    recon_mine = total(own(recon_pair, core, 1)).T.astype(BF16).reshape(n_rows_z, -1, half)
    bias_mine = own(dec_bias.reshape(2, half), core, 0)
    recon = total(exchange(recon_mine, ROWS_Z)) + bias_mine[None, :]
    count = recon.shape[0]
    both_recon = both_cores(recon.astype(BF16)).reshape(2, 2, count // 2, half)
    recon_out = own(both_recon, core, 1).transpose(1, 0, 2).reshape(count // 2, width)

    scale = 1.0 / math.sqrt(tokens)
    first = lax.axis_index(ROWS_Z) * count
    target = own(
        lax.dynamic_slice_in_dim(shuffled, first, count, 0).reshape(count, 2, half), core, 1
    )
    err_own = (scale * (recon - target.astype(F32))).astype(BF16)
    err_pair = both_cores(sent_to_all(err_own, ROWS_Z).reshape(tokens, half))
    d_err = jnp.concatenate([err_pair[0], err_pair[1]], axis=1)

    back_local = lax.dot_general(
        d_err, decoder, (((1,), (1,)), ((), ())), preferred_element_type=F32
    ).astype(BF16)
    d_latent = total(exchange(back_local.reshape(n_hidden, -1, latents), HIDDEN))
    grad_dec = lax.dot_general(
        latent_act, d_err, (((0,), (0,)), ((), ())), preferred_element_type=F32
    ).astype(BF16)
    d_pre_own = (
        (d_latent + sparsity_weight * scale) * jax.nn.sigmoid(pre_act / smooth_scale)
    ).astype(BF16)
    d_pre = sent_to_all(d_pre_own, HIDDEN).reshape(tokens, latents)
    grad_enc = jnp.dot(shuffled_t, d_pre, preferred_element_type=F32).astype(BF16)
    return (recon_out, grad_enc, grad_dec)


def solution(mesh):
    finer = Mesh(
        mesh.devices.reshape(mesh.shape["rows"], 2, 4, 16, 2),
        (R, Y, X, Z, C),
    )
    return jax.shard_map(
        shards,
        mesh=finer,
        in_specs=(
            P(R, HIDDEN_LATENTS),
            P(None, HIDDEN_LATENTS),
            P(None, HIDDEN_LATENTS),
            P(HIDDEN_LATENTS, None),
            P(HIDDEN, ROWS_LATENTS),
            P(ROWS_LATENTS, HIDDEN),
            P(ROWS_LATENTS),
            P(HIDDEN),
            P(),
        ),
        out_specs=(P(ROWS_LATENTS, HIDDEN), P(HIDDEN, ROWS_LATENTS), P(ROWS_LATENTS, HIDDEN)),
        check_vma=False,
    )
```

```python
import math

import jax
import jax.numpy as jnp
from jax import lax
from jax.sharding import Mesh
from jax.sharding import PartitionSpec as P

R, Y, X, Z, C = "rows", "hidden_0", "hidden_1", "latents_0", "latents_1"
HIDDEN = (Y, X)
LATENTS = (Z, C)
HIDDEN_LATENTS = (Y, X, Z, C)
ROWS_LATENTS = (R, Z, C)
ROWS_Z = (R, Z)
ROWS_HIDDEN = (R, Y, X)

smooth_scale = 0.1
sparsity_weight = 0.5
F32 = jnp.float32
BF16 = jnp.bfloat16


def exchange(blocks, axes):
    return lax.all_to_all(blocks, axes, 0, 0, tiled=True)


def sent_to_all(x, axes):
    return exchange(jnp.broadcast_to(x, (lax.axis_size(axes), *x.shape)), axes)


def both_cores(x):
    return lax.all_gather(x, C, axis=0, tiled=False)


def swapped(x, axis):
    return lax.ppermute(x, axis, [(0, 1), (1, 0)])


def total(blocks):
    return jnp.sum(blocks.astype(F32), axis=0)


def own(x, index, dim):
    return lax.dynamic_index_in_dim(x, index, dim, keepdims=False)


def shards(
    inputs, gate_weight, up_weight, down_weight, encoder, decoder, enc_bias, dec_bias, shuffle_order
):
    tokens = shuffle_order.shape[0]
    n_hidden = lax.axis_size(HIDDEN)
    n_z = lax.axis_size(Z)
    core = lax.axis_index(C)
    row = lax.axis_index(R)
    width = decoder.shape[1]
    half = width // 2
    latents = encoder.shape[1]
    units = gate_weight.shape[1]

    weights = lax.optimization_barrier(jnp.concatenate([gate_weight.T, up_weight.T], axis=0))
    few = sent_to_all(inputs.T, Z)

    few, down = lax.optimization_barrier((few, down_weight))
    blocks = down.reshape(units, n_hidden, 2, half)
    kept, given = own(blocks, core, 2), own(blocks, 1 - core, 2)
    taken = swapped(given, C)
    down_pair = jnp.concatenate(
        [jnp.where(core == 0, kept, taken), jnp.where(core == 0, taken, kept)]
    ).reshape(2 * units, n_hidden * half)

    every = both_cores(sent_to_all(few, HIDDEN))
    gathered = every.transpose(1, 2, 0, 3, 4).reshape(-1, inputs.shape[0])
    acts = jnp.dot(weights, gathered, preferred_element_type=F32)
    hidden = (jax.nn.gelu(acts[:units], approximate=True) * acts[units:]).astype(BF16)
    hidden_pair = both_cores(hidden).reshape(2 * units, -1)
    mine = lax.dot_general(
        down_pair, hidden_pair, (((0,), (0,)), ((), ())), preferred_element_type=F32
    ).astype(BF16).reshape(n_hidden, half, -1)

    summed = total(exchange(mine, HIDDEN)).T.astype(BF16)

    summed, decoder_own, bias_own = lax.optimization_barrier((summed, decoder, enc_bias))
    decoder_far, bias_far = swapped(decoder_own, R), swapped(bias_own, R)

    rows_own = total(exchange(summed.reshape(n_z, -1, half), Z)).astype(BF16)
    rows_all = sent_to_all(rows_own, ROWS_Z)
    rows_all, decoder_far, bias_far = lax.optimization_barrier((rows_all, decoder_far, bias_far))
    mlp_out = both_cores(rows_all.reshape(tokens, half))
    decoder_both = jnp.concatenate([decoder_own, decoder_far])
    bias_both = jnp.concatenate([bias_own, bias_far])
    low = row == 0

    pick = (shuffle_order[:, None] == jnp.arange(tokens)[None, :]).astype(BF16)
    shuffled = jnp.concatenate(
        [jnp.dot(pick, mlp_out[c], preferred_element_type=F32).astype(BF16) for c in range(2)],
        axis=1,
    )

    group = tokens // 2
    pre_local = jnp.dot(shuffled, encoder, preferred_element_type=F32).astype(BF16)
    pre_parts = exchange(pre_local.reshape(2 * n_hidden, -1, latents), ROWS_HIDDEN)
    pre_sums = jnp.sum(pre_parts.reshape(2, n_hidden, -1, latents).astype(F32), axis=1)
    pre_act = jnp.concatenate(
        [jnp.where(low, *pre_sums), jnp.where(low, pre_sums[1], pre_sums[0])], axis=1
    ) + bias_both[None, :]
    latent_own = (smooth_scale * jax.nn.softplus(pre_act / smooth_scale)).astype(BF16)
    latent_act = sent_to_all(latent_own, HIDDEN).reshape(group, 2 * latents)
    scale = 1.0 / math.sqrt(tokens)
    count = group // n_z
    first = lax.axis_index(ROWS_Z) * count
    target = own(
        lax.dynamic_slice_in_dim(shuffled, first, count, 0).reshape(count, 2, half), core, 1
    )
    bias_mine = own(dec_bias.reshape(2, half), core, 0)
    latent_act, decoder_both, target, bias_mine = lax.optimization_barrier(
        (latent_act, decoder_both, target, bias_mine)
    )
    recon_local = lax.dot_general(
        decoder_both, latent_act, (((0,), (1,)), ((), ())), preferred_element_type=F32
    ).astype(BF16)
    recon_pair = both_cores(recon_local).reshape(2, 2, half, group)
    recon_mine = total(own(recon_pair, core, 1)).T.astype(BF16).reshape(n_z, -1, half)
    recon = total(exchange(recon_mine, Z)) + bias_mine[None, :]
    err_own = (scale * (recon - target.astype(F32))).astype(BF16)
    err_pair = both_cores(sent_to_all(err_own, Z).reshape(group, half))
    d_err = jnp.concatenate([err_pair[0], err_pair[1]], axis=1)

    back_local = lax.dot_general(
        d_err, decoder_both, (((1,), (1,)), ((), ())), preferred_element_type=F32
    ).astype(BF16)
    d_latent = total(exchange(back_local.reshape(n_hidden, -1, 2 * latents), HIDDEN))
    d_pre_own = (
        (d_latent + sparsity_weight * scale) * jax.nn.sigmoid(pre_act / smooth_scale)
    ).astype(BF16)
    d_pre_near, d_pre_far = d_pre_own[:, :latents], d_pre_own[:, latents:]
    d_pre_cut = jnp.stack(
        [jnp.where(low, d_pre_near, d_pre_far), jnp.where(low, d_pre_far, d_pre_near)]
    )
    d_pre = exchange(
        jnp.broadcast_to(d_pre_cut[:, None], (2, n_hidden, *d_pre_cut.shape[1:])).reshape(
            2 * n_hidden, -1, latents
        ),
        ROWS_HIDDEN,
    ).reshape(tokens, latents)

    latent_all = jnp.concatenate(
        [latent_act[:, :latents], swapped(latent_act[:, latents:], R)]
    )
    err_all = jnp.concatenate([d_err, swapped(d_err, R)])
    grad_dec = lax.dot_general(
        latent_all, err_all, (((0,), (0,)), ((), ())), preferred_element_type=F32
    ).astype(BF16)
    grad_enc = lax.dot_general(
        shuffled, d_pre, (((0,), (0,)), ((), ())), preferred_element_type=F32
    ).astype(BF16)

    both_recon = both_cores(recon.astype(BF16)).reshape(2, 2, count // 2, half)
    recon_out = own(both_recon, core, 1).transpose(1, 0, 2).reshape(count // 2, width)
    return (recon_out, grad_enc, grad_dec)


def solution(mesh):
    finer = Mesh(
        mesh.devices.reshape(mesh.shape["rows"], 2, 4, 16, 2),
        (R, Y, X, Z, C),
    )
    return jax.shard_map(
        shards,
        mesh=finer,
        in_specs=(
            P(R, HIDDEN_LATENTS),
            P(None, HIDDEN_LATENTS),
            P(None, HIDDEN_LATENTS),
            P(HIDDEN_LATENTS, None),
            P(HIDDEN, ROWS_LATENTS),
            P(ROWS_LATENTS, HIDDEN),
            P(ROWS_LATENTS),
            P(HIDDEN),
            P(),
        ),
        out_specs=(P(ROWS_LATENTS, HIDDEN), P(HIDDEN, ROWS_LATENTS), P(ROWS_LATENTS, HIDDEN)),
        check_vma=False,
    )
```

```python
import math

import jax
import jax.numpy as jnp
from jax import lax
from jax.sharding import Mesh
from jax.sharding import PartitionSpec as P

R, Y, X, Z, C = "rows", "hidden_0", "hidden_1", "latents_0", "latents_1"
HIDDEN = (Y, X)
LATENTS = (Z, C)
HIDDEN_LATENTS = (Y, X, Z, C)
ROWS_LATENTS = (R, Z, C)
ROWS_Z = (R, Z)
ROWS_HIDDEN = (R, Y, X)

smooth_scale = 0.1
sparsity_weight = 0.5
F32 = jnp.float32
BF16 = jnp.bfloat16


def exchange(blocks, axes):
    return lax.all_to_all(blocks, axes, 0, 0, tiled=True)


def sent_to_all(x, axes):
    return exchange(jnp.broadcast_to(x, (lax.axis_size(axes), *x.shape)), axes)


def both_cores(x):
    return lax.all_gather(x, C, axis=0, tiled=False)


def both_rows(x):
    return lax.all_gather(x, R, axis=0, tiled=False)


def tied(*arrays):
    return lax.optimization_barrier(arrays)


def total(blocks):
    return jnp.sum(blocks.astype(F32), axis=0)


def own(x, index, dim):
    return lax.dynamic_index_in_dim(x, index, dim, keepdims=False)


def shards(
    inputs, gate_weight, up_weight, down_weight, encoder, decoder, enc_bias, dec_bias, shuffle_order
):
    tokens = shuffle_order.shape[0]
    n_hidden = lax.axis_size(HIDDEN)
    n_z = lax.axis_size(Z)
    core = lax.axis_index(C)
    row = lax.axis_index(R)
    width = decoder.shape[1]
    half = width // 2
    latents = encoder.shape[1]
    units = gate_weight.shape[1]

    low = row == 0

    mine, gate_own, up_own, bias_own, out_bias = tied(
        inputs.T, gate_weight, up_weight, enc_bias, dec_bias
    )
    few = sent_to_all(mine, Z)
    weights = jnp.concatenate([gate_own.T, up_own.T], axis=0)
    bias_both = jnp.concatenate([bias_own, own(both_rows(bias_own), 1 - row, 0)])
    bias_mine = own(out_bias.reshape(2, half), core, 0)
    few, weights, bias_both, bias_mine = tied(few, weights, bias_both, bias_mine)

    few, down_own = tied(few, down_weight)
    more = sent_to_all(few, HIDDEN)
    down_pair = own(both_cores(down_own).reshape(2 * units, n_hidden, 2, half), core, 2)
    more, down_pair = tied(more, down_pair.reshape(2 * units, n_hidden * half))

    every = both_cores(more)
    gathered = every.transpose(1, 2, 0, 3, 4).reshape(-1, inputs.shape[0])
    acts = jnp.dot(weights, gathered, preferred_element_type=F32)
    hidden = (jax.nn.gelu(acts[:units], approximate=True) * acts[units:]).astype(BF16)
    hidden_pair = both_cores(hidden).reshape(2 * units, -1)
    mine = lax.dot_general(
        down_pair, hidden_pair, (((0,), (0,)), ((), ())), preferred_element_type=F32
    ).astype(BF16).reshape(n_hidden, half, -1)

    summed = total(exchange(mine, HIDDEN)).T.astype(BF16)

    decoder_t = decoder.T
    summed, decoder_left = tied(summed, decoder_t[:half])
    row_parts = exchange(summed.reshape(n_z, -1, half), Z)
    decoder_left = both_rows(decoder_left)
    row_parts, decoder_left = tied(row_parts, decoder_left)
    rows_own = total(row_parts).astype(BF16)
    rows_own, decoder_right = tied(rows_own, decoder_t[half:])
    rows_all = sent_to_all(rows_own, ROWS_Z)
    decoder_right = both_rows(decoder_right)
    rows_all, decoder_right = tied(rows_all, decoder_right)
    mlp_out = both_cores(rows_all.reshape(tokens, half))

    def picked(order):
        return (order[:, None] == jnp.arange(tokens)[None, :]).astype(BF16)

    scale = 1.0 / math.sqrt(tokens)
    group = tokens // 2
    count = group // n_z
    order_own = lax.dynamic_slice_in_dim(shuffle_order, lax.axis_index(ROWS_Z) * count, count, 0)
    target = jnp.dot(picked(order_own), own(mlp_out, core, 0), preferred_element_type=F32)
    mlp_out, target = tied(mlp_out, target)
    pick = picked(shuffle_order)
    shuffled = jnp.concatenate(
        [jnp.dot(pick, mlp_out[c], preferred_element_type=F32).astype(BF16) for c in range(2)],
        axis=1,
    )

    pre_local = jnp.dot(shuffled, encoder, preferred_element_type=F32).astype(BF16)
    pre_parts = exchange(pre_local.reshape(2 * n_hidden, -1, latents), ROWS_HIDDEN)
    pre_sums = jnp.sum(pre_parts.reshape(2, n_hidden, -1, latents).astype(F32), axis=1)
    pre_act = jnp.concatenate(
        [jnp.where(low, *pre_sums), jnp.where(low, pre_sums[1], pre_sums[0])], axis=1
    ) + bias_both[None, :]
    latent_own = (smooth_scale * jax.nn.softplus(pre_act / smooth_scale)).astype(BF16)
    latent_own, decoder_left, decoder_right, pre_act = tied(
        latent_own, decoder_left, decoder_right, pre_act
    )
    latent_act = sent_to_all(latent_own, HIDDEN).reshape(group, 2 * latents)
    decoder_far = jnp.concatenate([own(decoder_left, 1 - row, 0), own(decoder_right, 1 - row, 0)])
    decoder_both = jnp.concatenate([decoder_t, decoder_far], axis=1)
    slope = jax.nn.sigmoid(pre_act / smooth_scale)
    latent_act, decoder_both, slope = tied(latent_act, decoder_both, slope)
    recon_local = lax.dot_general(
        decoder_both, latent_act, (((1,), (1,)), ((), ())), preferred_element_type=F32
    ).astype(BF16)
    recon_pair = both_cores(recon_local).reshape(2, 2, half, group)
    recon_mine = total(own(recon_pair, core, 1)).T.astype(BF16).reshape(n_z, -1, half)
    recon_mine, latent_far = tied(recon_mine, latent_act[:, latents:])
    recon_parts = exchange(recon_mine, Z)
    latent_far = own(both_rows(latent_far), 1 - row, 0)
    recon_parts, latent_far = tied(recon_parts, latent_far)
    recon = total(recon_parts) + bias_mine[None, :]
    err_own = (scale * (recon - target)).astype(BF16)
    err_pair = both_cores(sent_to_all(err_own, Z).reshape(group, half))
    d_err = jnp.concatenate([err_pair[0], err_pair[1]], axis=1)

    back_local = jnp.dot(d_err, decoder_both, preferred_element_type=F32).astype(BF16)
    back_local, err_near = tied(back_local, err_pair)
    back_parts = exchange(back_local.reshape(n_hidden, -1, 2 * latents), HIDDEN)
    err_far = own(both_rows(err_near), 1 - row, 0)
    err_far = jnp.concatenate([err_far[0], err_far[1]], axis=1)
    back_parts, err_far = tied(back_parts, err_far)
    d_latent = total(back_parts)
    d_pre_own = ((d_latent + sparsity_weight * scale) * slope).astype(BF16)
    d_pre_near, d_pre_far = d_pre_own[:, :latents], d_pre_own[:, latents:]
    d_pre_cut = jnp.stack(
        [jnp.where(low, d_pre_near, d_pre_far), jnp.where(low, d_pre_far, d_pre_near)]
    )
    d_pre = exchange(
        jnp.broadcast_to(d_pre_cut[:, None], (2, n_hidden, *d_pre_cut.shape[1:])).reshape(
            2 * n_hidden, -1, latents
        ),
        ROWS_HIDDEN,
    ).reshape(tokens, latents)

    latent_all = jnp.concatenate([latent_act[:, :latents], latent_far])
    err_all = jnp.concatenate([d_err, err_far])
    grad_dec = lax.dot_general(
        latent_all, err_all, (((0,), (0,)), ((), ())), preferred_element_type=F32
    ).astype(BF16)
    grad_enc = lax.dot_general(
        shuffled, d_pre, (((0,), (0,)), ((), ())), preferred_element_type=F32
    ).astype(BF16)

    both_recon = both_cores(recon.astype(BF16)).reshape(2, 2, count // 2, half)
    recon_out = own(both_recon, core, 1).transpose(1, 0, 2).reshape(count // 2, width)
    return (recon_out, grad_enc, grad_dec)


def solution(mesh):
    finer = Mesh(
        mesh.devices.reshape(mesh.shape["rows"], 2, 4, 16, 2),
        (R, Y, X, Z, C),
    )
    return jax.shard_map(
        shards,
        mesh=finer,
        in_specs=(
            P(R, HIDDEN_LATENTS),
            P(None, HIDDEN_LATENTS),
            P(None, HIDDEN_LATENTS),
            P(HIDDEN_LATENTS, None),
            P(HIDDEN, ROWS_LATENTS),
            P(ROWS_LATENTS, HIDDEN),
            P(ROWS_LATENTS),
            P(HIDDEN),
            P(),
        ),
        out_specs=(P(ROWS_LATENTS, HIDDEN), P(HIDDEN, ROWS_LATENTS), P(ROWS_LATENTS, HIDDEN)),
        check_vma=False,
    )
```

```python
import math

import jax
import jax.numpy as jnp
from jax import lax
from jax.sharding import Mesh
from jax.sharding import PartitionSpec as P

R, Y, X, Z, C = "rows", "hidden_0", "hidden_1", "latents_0", "latents_1"
HIDDEN = (Y, X)
LATENTS = (Z, C)
HIDDEN_LATENTS = (Y, X, Z, C)
ROWS_LATENTS = (R, Z, C)
ROWS_Z = (R, Z)
ROWS_HIDDEN = (R, Y, X)

smooth_scale = 0.1
sparsity_weight = 0.5
F32 = jnp.float32
BF16 = jnp.bfloat16


def exchange(blocks, axes):
    return lax.all_to_all(blocks, axes, 0, 0, tiled=True)


def sent_to_all(x, axes):
    return exchange(jnp.broadcast_to(x, (lax.axis_size(axes), *x.shape)), axes)


def both_cores(x):
    return lax.all_gather(x, C, axis=0, tiled=False)


def swapped_rows(x):
    return lax.ppermute(x, R, [(0, 1), (1, 0)])


def both_rows(x):
    return lax.all_gather(x, R, axis=0, tiled=False)


def tied(*arrays):
    return lax.optimization_barrier(arrays)


def total(blocks):
    return jnp.sum(blocks.astype(F32), axis=0)


def own(x, index, dim):
    return lax.dynamic_index_in_dim(x, index, dim, keepdims=False)


def shards(
    inputs, gate_weight, up_weight, down_weight, encoder, decoder, enc_bias, dec_bias, shuffle_order
):
    tokens = shuffle_order.shape[0]
    n_hidden = lax.axis_size(HIDDEN)
    n_z = lax.axis_size(Z)
    core = lax.axis_index(C)
    row = lax.axis_index(R)
    width = decoder.shape[1]
    half = width // 2
    latents = encoder.shape[1]
    units = gate_weight.shape[1]

    low = row == 0

    mine, gate_own, up_own, bias_own, out_bias = tied(
        inputs.T, gate_weight, up_weight, enc_bias, dec_bias
    )
    few = sent_to_all(mine, Z)
    weights = jnp.concatenate([gate_own.T, up_own.T], axis=0)
    bias_both = jnp.concatenate([bias_own, own(both_rows(bias_own), 1 - row, 0)])
    bias_mine = own(out_bias.reshape(2, half), core, 0)
    few, weights, bias_both, bias_mine = tied(few, weights, bias_both, bias_mine)

    few, down_own = tied(few, down_weight)
    more = sent_to_all(few, HIDDEN)
    more, down_pair = tied(more, both_cores(down_own).reshape(2 * units, -1))

    every = both_cores(more)
    gathered = every.transpose(1, 2, 0, 3, 4).reshape(-1, inputs.shape[0])
    acts = jnp.dot(weights, gathered, preferred_element_type=F32)
    hidden = (jax.nn.gelu(acts[:units], approximate=True) * acts[units:]).astype(BF16)
    hidden_pair = both_cores(hidden).reshape(2 * units, -1)
    mine = lax.dot_general(
        down_pair, hidden_pair, (((0,), (0,)), ((), ())), preferred_element_type=F32
    ).astype(BF16)
    mine = own(mine.reshape(n_hidden, 2, half, -1), core, 1)

    summed = total(exchange(mine, HIDDEN)).T.astype(BF16)

    summed, decoder_near = tied(summed, decoder.T)
    decoder_far = swapped_rows(decoder_near)
    rows_own = total(exchange(summed.reshape(n_z, -1, half), Z)).astype(BF16)
    rows_all = sent_to_all(rows_own, ROWS_Z)
    rows_all, decoder_far = tied(rows_all, decoder_far)
    mlp_out = both_cores(rows_all.reshape(tokens, half))

    def picked(order):
        return (order[:, None] == jnp.arange(tokens)[None, :]).astype(BF16)

    scale = 1.0 / math.sqrt(tokens)
    group = tokens // 2
    count = group // n_z
    order_own = lax.dynamic_slice_in_dim(shuffle_order, lax.axis_index(ROWS_Z) * count, count, 0)
    target = jnp.dot(picked(order_own), own(mlp_out, core, 0), preferred_element_type=F32)
    mlp_out, target = tied(mlp_out, target)
    pick = picked(shuffle_order)
    shuffled = jnp.concatenate(
        [jnp.dot(pick, mlp_out[c], preferred_element_type=F32).astype(BF16) for c in range(2)],
        axis=1,
    )

    pre_local = jnp.dot(shuffled, encoder, preferred_element_type=F32).astype(BF16)
    pre_parts = exchange(pre_local.reshape(2 * n_hidden, -1, latents), ROWS_HIDDEN)
    pre_sums = jnp.sum(pre_parts.reshape(2, n_hidden, -1, latents).astype(F32), axis=1)
    pre_act = jnp.concatenate(
        [jnp.where(low, *pre_sums), jnp.where(low, pre_sums[1], pre_sums[0])], axis=1
    ) + bias_both[None, :]
    latent_own = (smooth_scale * jax.nn.softplus(pre_act / smooth_scale)).astype(BF16)
    latent_own, decoder_far, pre_act = tied(latent_own, decoder_far, pre_act)
    latent_act = sent_to_all(latent_own, HIDDEN).reshape(group, 2 * latents)
    decoder_both = jnp.concatenate([decoder_near, decoder_far], axis=1)
    slope = jax.nn.sigmoid(pre_act / smooth_scale)
    latent_act, decoder_both, slope = tied(latent_act, decoder_both, slope)
    recon_local = lax.dot_general(
        decoder_both, latent_act, (((1,), (1,)), ((), ())), preferred_element_type=F32
    ).astype(BF16)
    recon_pair = both_cores(recon_local).reshape(2, 2, half, group)
    recon_mine = total(own(recon_pair, core, 1)).T.astype(BF16).reshape(n_z, -1, half)
    recon_parts = exchange(recon_mine, Z)
    recon = total(recon_parts) + bias_mine[None, :]
    err_own = (scale * (recon - target)).astype(BF16)
    err_pair = both_cores(sent_to_all(err_own, Z).reshape(group, half))
    d_err = jnp.concatenate([err_pair[0], err_pair[1]], axis=1)

    back_local = jnp.dot(d_err, decoder_both, preferred_element_type=F32).astype(BF16)
    back_local, err_near, latent_far = tied(back_local, d_err, latent_act[:, latents:])
    back_parts = exchange(back_local.reshape(n_hidden, -1, 2 * latents), HIDDEN)
    back_parts, err_far, latent_far = tied(
        back_parts, swapped_rows(err_near), swapped_rows(latent_far)
    )
    d_latent = total(back_parts)
    d_pre_own = ((d_latent + sparsity_weight * scale) * slope).astype(BF16)
    d_pre_near, d_pre_far = d_pre_own[:, :latents], d_pre_own[:, latents:]
    d_pre_cut = jnp.stack(
        [jnp.where(low, d_pre_near, d_pre_far), jnp.where(low, d_pre_far, d_pre_near)]
    )
    d_pre = exchange(
        jnp.broadcast_to(d_pre_cut[:, None], (2, n_hidden, *d_pre_cut.shape[1:])).reshape(
            2 * n_hidden, -1, latents
        ),
        ROWS_HIDDEN,
    ).reshape(tokens, latents)

    latent_all = jnp.concatenate([latent_act[:, :latents], latent_far])
    err_all = jnp.concatenate([d_err, err_far])
    grad_dec = lax.dot_general(
        latent_all, err_all, (((0,), (0,)), ((), ())), preferred_element_type=F32
    ).astype(BF16)
    grad_enc = lax.dot_general(
        shuffled, d_pre, (((0,), (0,)), ((), ())), preferred_element_type=F32
    ).astype(BF16)

    both_recon = both_cores(recon.astype(BF16)).reshape(2, 2, count // 2, half)
    recon_out = own(both_recon, core, 1).transpose(1, 0, 2).reshape(count // 2, width)
    return (recon_out, grad_enc, grad_dec)


def solution(mesh):
    finer = Mesh(
        mesh.devices.reshape(mesh.shape["rows"], 2, 4, 16, 2),
        (R, Y, X, Z, C),
    )
    return jax.shard_map(
        shards,
        mesh=finer,
        in_specs=(
            P(R, HIDDEN_LATENTS),
            P(None, HIDDEN_LATENTS),
            P(None, HIDDEN_LATENTS),
            P(HIDDEN_LATENTS, None),
            P(HIDDEN, ROWS_LATENTS),
            P(ROWS_LATENTS, HIDDEN),
            P(ROWS_LATENTS),
            P(HIDDEN),
            P(),
        ),
        out_specs=(P(ROWS_LATENTS, HIDDEN), P(HIDDEN, ROWS_LATENTS), P(ROWS_LATENTS, HIDDEN)),
        check_vma=False,
    )
```

```python
import math

import jax
import jax.numpy as jnp
from jax import lax
from jax.sharding import Mesh
from jax.sharding import PartitionSpec as P

R, Y, X, Z, C = "rows", "hidden_0", "hidden_1", "latents_0", "latents_1"
HIDDEN = (Y, X)
LATENTS = (Z, C)
HIDDEN_LATENTS = (Y, X, Z, C)
ROWS_LATENTS = (R, Z, C)
ROWS_Z = (R, Z)

smooth_scale = 0.1
sparsity_weight = 0.5
F32 = jnp.float32
BF16 = jnp.bfloat16


def exchange(blocks, axes):
    return lax.all_to_all(blocks, axes, 0, 0, tiled=True)


def sent_to_all(x, axes):
    return exchange(jnp.broadcast_to(x, (lax.axis_size(axes), *x.shape)), axes)


def both_cores(x):
    return lax.all_gather(x, C, axis=0, tiled=False)


def tied(*arrays):
    return lax.optimization_barrier(arrays)


def total(blocks):
    return jnp.sum(blocks.astype(F32), axis=0)


def own(x, index, dim):
    return lax.dynamic_index_in_dim(x, index, dim, keepdims=False)


def shards(
    inputs, gate_weight, up_weight, down_weight, encoder, decoder, enc_bias, dec_bias, shuffle_order
):
    tokens = shuffle_order.shape[0]
    n_hidden = lax.axis_size(HIDDEN)
    n_z = lax.axis_size(Z)
    n_rows_z = lax.axis_size(ROWS_Z)
    core = lax.axis_index(C)
    width = decoder.shape[1]
    half = width // 2
    latents = encoder.shape[1]
    units = gate_weight.shape[1]

    few = sent_to_all(inputs.T, Z)
    few, gate_own, up_own, down_own, out_bias = tied(
        few, gate_weight, up_weight, down_weight, dec_bias
    )
    more = sent_to_all(few, HIDDEN)
    weights = jnp.concatenate([gate_own.T, up_own.T], axis=0)
    down_pair = both_cores(down_own).reshape(2 * units, -1)
    bias_mine = own(out_bias.reshape(2, half), core, 0)
    more, weights, down_pair, bias_mine = tied(more, weights, down_pair, bias_mine)
    every = both_cores(more)
    gathered = every.transpose(1, 2, 0, 3, 4).reshape(-1, inputs.shape[0])
    acts = jnp.dot(weights, gathered, preferred_element_type=F32)
    hidden = (jax.nn.gelu(acts[:units], approximate=True) * acts[units:]).astype(BF16)
    hidden_pair = both_cores(hidden).reshape(2 * units, -1)
    mine = lax.dot_general(
        down_pair, hidden_pair, (((0,), (0,)), ((), ())), preferred_element_type=F32
    ).astype(BF16)
    mine = own(mine.reshape(n_hidden, 2, half, -1), core, 1)

    summed = total(exchange(mine, HIDDEN)).T.astype(BF16)
    rows_own = total(exchange(summed.reshape(n_z, -1, half), Z)).astype(BF16)
    mlp_out = both_cores(sent_to_all(rows_own, ROWS_Z).reshape(tokens, half))

    def picked(order):
        return (order[:, None] == jnp.arange(tokens)[None, :]).astype(BF16)

    scale = 1.0 / math.sqrt(tokens)
    count = tokens // n_rows_z
    order_own = lax.dynamic_slice_in_dim(shuffle_order, lax.axis_index(ROWS_Z) * count, count, 0)
    target = jnp.dot(picked(order_own), own(mlp_out, core, 0), preferred_element_type=F32)
    mlp_out, target = tied(mlp_out, target)
    pick = picked(shuffle_order)
    shuffled = jnp.concatenate(
        [jnp.dot(pick, mlp_out[c], preferred_element_type=F32).astype(BF16) for c in range(2)],
        axis=1,
    )
    pre_local = jnp.dot(shuffled, encoder, preferred_element_type=F32).astype(BF16)
    pre_act = total(exchange(pre_local.reshape(n_hidden, -1, latents), HIDDEN)) + enc_bias[None, :]
    latent_own = (smooth_scale * jax.nn.softplus(pre_act / smooth_scale)).astype(BF16)
    latent_act = sent_to_all(latent_own, HIDDEN).reshape(tokens, latents)
    recon_local = lax.dot_general(
        decoder, latent_act, (((0,), (1,)), ((), ())), preferred_element_type=F32
    ).astype(BF16)
    recon_pair = both_cores(recon_local).reshape(2, 2, half, tokens)
    recon_mine = total(own(recon_pair, core, 1)).T.astype(BF16).reshape(n_rows_z, -1, half)
    recon = total(exchange(recon_mine, ROWS_Z)) + bias_mine[None, :]
    err_own = (scale * (recon - target)).astype(BF16)
    err_pair = both_cores(sent_to_all(err_own, ROWS_Z).reshape(tokens, half))
    d_err = jnp.concatenate([err_pair[0], err_pair[1]], axis=1)

    back_local = lax.dot_general(
        d_err, decoder, (((1,), (1,)), ((), ())), preferred_element_type=F32
    ).astype(BF16)
    d_latent = total(exchange(back_local.reshape(n_hidden, -1, latents), HIDDEN))
    grad_dec = lax.dot_general(
        latent_act, d_err, (((0,), (0,)), ((), ())), preferred_element_type=F32
    ).astype(BF16)
    d_pre_own = (
        (d_latent + sparsity_weight * scale) * jax.nn.sigmoid(pre_act / smooth_scale)
    ).astype(BF16)
    d_pre = sent_to_all(d_pre_own, HIDDEN).reshape(tokens, latents)
    grad_enc = lax.dot_general(
        shuffled, d_pre, (((0,), (0,)), ((), ())), preferred_element_type=F32
    ).astype(BF16)
    both_recon = both_cores(recon.astype(BF16)).reshape(2, 2, count // 2, half)
    recon_out = own(both_recon, core, 1).transpose(1, 0, 2).reshape(count // 2, width)
    return (recon_out, grad_enc, grad_dec)


def solution(mesh):
    finer = Mesh(
        mesh.devices.reshape(mesh.shape["rows"], 2, 4, 16, 2),
        (R, Y, X, Z, C),
    )
    return jax.shard_map(
        shards,
        mesh=finer,
        in_specs=(
            P(R, HIDDEN_LATENTS),
            P(None, HIDDEN_LATENTS),
            P(None, HIDDEN_LATENTS),
            P(HIDDEN_LATENTS, None),
            P(HIDDEN, ROWS_LATENTS),
            P(ROWS_LATENTS, HIDDEN),
            P(ROWS_LATENTS),
            P(HIDDEN),
            P(),
        ),
        out_specs=(P(ROWS_LATENTS, HIDDEN), P(HIDDEN, ROWS_LATENTS), P(ROWS_LATENTS, HIDDEN)),
        check_vma=False,
    )
```

```python
import math

import jax
import jax.numpy as jnp
from jax import lax
from jax.sharding import Mesh
from jax.sharding import PartitionSpec as P

R, Y, X, Z, C = "rows", "hidden_0", "hidden_1", "latents_0", "latents_1"
HIDDEN = (Y, X)
LATENTS = (Z, C)
HIDDEN_LATENTS = (Y, X, Z, C)
ROWS_LATENTS = (R, Z, C)
ROWS_Z = (R, Z)

smooth_scale = 0.1
sparsity_weight = 0.5
F32 = jnp.float32
BF16 = jnp.bfloat16


def exchange(blocks, axes):
    return lax.all_to_all(blocks, axes, 0, 0, tiled=True)


def copies_of(x, axes):
    return jnp.broadcast_to(x, (lax.axis_size(axes), *x.shape))


def sent_to_all(x, axes):
    return exchange(copies_of(x, axes), axes)


def both_cores(x):
    return lax.all_gather(x, C, axis=0, tiled=False)


def tied(*arrays):
    return lax.optimization_barrier(arrays)


def total(blocks):
    return jnp.sum(blocks.astype(F32), axis=0)


def own(x, index, dim):
    return lax.dynamic_index_in_dim(x, index, dim, keepdims=False)


def shards(
    inputs, gate_weight, up_weight, down_weight, encoder, decoder, enc_bias, dec_bias, shuffle_order
):
    tokens = shuffle_order.shape[0]
    n_hidden = lax.axis_size(HIDDEN)
    n_z = lax.axis_size(Z)
    n_rows_z = lax.axis_size(ROWS_Z)
    core = lax.axis_index(C)
    width = decoder.shape[1]
    half = width // 2
    latents = encoder.shape[1]
    units = gate_weight.shape[1]

    few = sent_to_all(inputs.T, Z)
    copies, gate_own, up_own, down_own, order, out_bias = tied(
        copies_of(few, HIDDEN), gate_weight, up_weight, down_weight, shuffle_order, dec_bias
    )
    more = exchange(copies, HIDDEN)
    weights = jnp.concatenate([gate_own.T, up_own.T], axis=0)
    down_pair = both_cores(down_own).reshape(2 * units, -1)
    count = tokens // n_rows_z
    order_own = lax.dynamic_slice_in_dim(order, lax.axis_index(ROWS_Z) * count, count, 0)
    bias_mine = lax.dynamic_slice_in_dim(out_bias, core * half, half, 0)
    more, weights, down_pair, order_own, bias_mine = tied(
        more, weights, down_pair, order_own, bias_mine
    )
    every = both_cores(more)
    gathered = every.transpose(1, 2, 0, 3, 4).reshape(-1, inputs.shape[0])
    acts = jnp.dot(weights, gathered, preferred_element_type=F32)
    hidden = (jax.nn.gelu(acts[:units], approximate=True) * acts[units:]).astype(BF16)
    hidden_pair = both_cores(hidden).reshape(2 * units, -1)
    mine = lax.dot_general(
        down_pair, hidden_pair, (((0,), (0,)), ((), ())), preferred_element_type=F32
    ).astype(BF16)
    mine = own(mine.reshape(n_hidden, 2, half, -1), core, 1)

    summed = total(exchange(mine, HIDDEN)).T.astype(BF16)
    rows_own = total(exchange(summed.reshape(n_z, -1, half), Z)).astype(BF16)
    mlp_out = both_cores(sent_to_all(rows_own, ROWS_Z).reshape(tokens, half))

    def picked(order):
        return (order[:, None] == jnp.arange(tokens)[None, :]).astype(BF16)

    scale = 1.0 / math.sqrt(tokens)
    target = jnp.dot(picked(order_own), own(mlp_out, core, 0), preferred_element_type=F32)
    mlp_out, target = tied(mlp_out, target)
    pick = picked(shuffle_order)
    shuffled = jnp.concatenate(
        [jnp.dot(pick, mlp_out[c], preferred_element_type=F32).astype(BF16) for c in range(2)],
        axis=1,
    )
    pre_local = jnp.dot(shuffled, encoder, preferred_element_type=F32).astype(BF16)
    pre_act = total(exchange(pre_local.reshape(n_hidden, -1, latents), HIDDEN)) + enc_bias[None, :]
    latent_own = (smooth_scale * jax.nn.softplus(pre_act / smooth_scale)).astype(BF16)
    latent_act = sent_to_all(latent_own, HIDDEN).reshape(tokens, latents)
    recon_local = lax.dot_general(
        decoder, latent_act, (((0,), (1,)), ((), ())), preferred_element_type=F32
    ).astype(BF16)
    recon_pair = both_cores(recon_local).reshape(2, 2, half, tokens)
    recon_mine = total(own(recon_pair, core, 1)).T.astype(BF16).reshape(n_rows_z, -1, half)
    recon = total(exchange(recon_mine, ROWS_Z)) + bias_mine[None, :]
    err_own = (scale * (recon - target)).astype(BF16)
    err_pair = both_cores(sent_to_all(err_own, ROWS_Z).reshape(tokens, half))
    d_err = jnp.concatenate([err_pair[0], err_pair[1]], axis=1)

    back_local = lax.dot_general(
        d_err, decoder, (((1,), (1,)), ((), ())), preferred_element_type=F32
    ).astype(BF16)
    d_latent = total(exchange(back_local.reshape(n_hidden, -1, latents), HIDDEN))
    grad_dec = lax.dot_general(
        latent_act, d_err, (((0,), (0,)), ((), ())), preferred_element_type=F32
    ).astype(BF16)
    d_pre_own = (
        (d_latent + sparsity_weight * scale) * jax.nn.sigmoid(pre_act / smooth_scale)
    ).astype(BF16)
    d_pre = sent_to_all(d_pre_own, HIDDEN).reshape(tokens, latents)
    grad_enc = lax.dot_general(
        shuffled, d_pre, (((0,), (0,)), ((), ())), preferred_element_type=F32
    ).astype(BF16)
    both_recon = both_cores(recon.astype(BF16)).reshape(2, 2, count // 2, half)
    recon_out = own(both_recon, core, 1).transpose(1, 0, 2).reshape(count // 2, width)
    return (recon_out, grad_enc, grad_dec)


def solution(mesh):
    finer = Mesh(
        mesh.devices.reshape(mesh.shape["rows"], 2, 4, 16, 2),
        (R, Y, X, Z, C),
    )
    return jax.shard_map(
        shards,
        mesh=finer,
        in_specs=(
            P(R, HIDDEN_LATENTS),
            P(None, HIDDEN_LATENTS),
            P(None, HIDDEN_LATENTS),
            P(HIDDEN_LATENTS, None),
            P(HIDDEN, ROWS_LATENTS),
            P(ROWS_LATENTS, HIDDEN),
            P(ROWS_LATENTS),
            P(HIDDEN),
            P(),
        ),
        out_specs=(P(ROWS_LATENTS, HIDDEN), P(HIDDEN, ROWS_LATENTS), P(ROWS_LATENTS, HIDDEN)),
        check_vma=False,
    )
```

```python
import math

import jax
import jax.numpy as jnp
from jax import lax
from jax.experimental import pallas as pl
from jax.experimental.pallas import tpu as pltpu
from jax.sharding import Mesh
from jax.sharding import PartitionSpec as P

R, Y, X, Z, C = "rows", "hidden_0", "hidden_1", "latents_0", "latents_1"
HIDDEN = (Y, X)
LATENTS = (Z, C)
HIDDEN_LATENTS = (Y, X, Z, C)
ROWS_LATENTS = (R, Z, C)
ROWS_Z = (R, Z)

smooth_scale = 0.1
sparsity_weight = 0.5
F32 = jnp.float32
BF16 = jnp.bfloat16


def exchange(blocks, axes):
    return lax.all_to_all(blocks, axes, 0, 0, tiled=True)


def copies_of(x, axes):
    return jnp.broadcast_to(x, (lax.axis_size(axes), *x.shape))


def sent_to_all(x, axes):
    return exchange(copies_of(x, axes), axes)


def both_cores(x):
    return lax.all_gather(x, C, axis=0, tiled=False)


def tied(*arrays):
    return lax.optimization_barrier(arrays)


def total(blocks):
    return jnp.sum(blocks.astype(F32), axis=0)


def own(x, index, dim):
    return lax.dynamic_index_in_dim(x, index, dim, keepdims=False)


def gated_kernel(gate_ref, up_ref, x_ref, hidden_ref):
    gate_act = jnp.dot(gate_ref[...], x_ref[...], preferred_element_type=F32)
    up_act = jnp.dot(up_ref[...], x_ref[...], preferred_element_type=F32)
    hidden_ref[...] = (jax.nn.gelu(gate_act, approximate=True) * up_act).astype(BF16)


def gated(gate, up, x):
    units, width = gate.shape
    count = x.shape[1]
    whole = pl.BlockSpec(memory_space=pltpu.VMEM)
    return pl.pallas_call(
        gated_kernel,
        in_specs=[whole] * 3,
        out_specs=whole,
        out_shape=jax.ShapeDtypeStruct((units, count), BF16),
        compiler_params=pltpu.CompilerParams(vmem_limit_bytes=16 * 2**20),
        cost_estimate=pl.CostEstimate(
            flops=4 * units * width * count,
            bytes_accessed=2 * width * (2 * units + count),
            transcendentals=units * count,
        ),
    )(gate, up, x)


def shards(
    inputs, gate_weight, up_weight, down_weight, encoder, decoder, enc_bias, dec_bias, shuffle_order
):
    tokens = shuffle_order.shape[0]
    n_hidden = lax.axis_size(HIDDEN)
    n_z = lax.axis_size(Z)
    n_rows_z = lax.axis_size(ROWS_Z)
    core = lax.axis_index(C)
    width = decoder.shape[1]
    half = width // 2
    latents = encoder.shape[1]
    units = gate_weight.shape[1]

    few = sent_to_all(inputs.T, Z)
    copies, gate_own, up_own, down_own, order, out_bias = tied(
        copies_of(few, HIDDEN), gate_weight, up_weight, down_weight, shuffle_order, dec_bias
    )
    more = exchange(copies, HIDDEN)
    down_pair = both_cores(down_own).reshape(2 * units, -1)
    count = tokens // n_rows_z
    order_own = lax.dynamic_slice_in_dim(order, lax.axis_index(ROWS_Z) * count, count, 0)
    bias_mine = lax.dynamic_slice_in_dim(out_bias, core * half, half, 0)
    more, gate_own, up_own, down_pair, order_own, bias_mine = tied(
        more, gate_own, up_own, down_pair, order_own, bias_mine
    )
    every = both_cores(more)
    gathered = every.transpose(1, 2, 0, 3, 4).reshape(-1, inputs.shape[0])
    hidden = gated(gate_own.T, up_own.T, gathered)
    hidden_pair = both_cores(hidden).reshape(2 * units, -1)
    mine = lax.dot_general(
        down_pair, hidden_pair, (((0,), (0,)), ((), ())), preferred_element_type=F32
    ).astype(BF16)
    mine = own(mine.reshape(n_hidden, 2, half, -1), core, 1)

    summed = total(exchange(mine, HIDDEN)).T.astype(BF16)
    rows_own = total(exchange(summed.reshape(n_z, -1, half), Z)).astype(BF16)
    mlp_out = both_cores(sent_to_all(rows_own, ROWS_Z).reshape(tokens, half))

    def picked(order):
        return (order[:, None] == jnp.arange(tokens)[None, :]).astype(BF16)

    scale = 1.0 / math.sqrt(tokens)
    target = jnp.dot(picked(order_own), own(mlp_out, core, 0), preferred_element_type=F32)
    mlp_out, target = tied(mlp_out, target)
    pick = picked(shuffle_order)
    shuffled = jnp.concatenate(
        [jnp.dot(pick, mlp_out[c], preferred_element_type=F32).astype(BF16) for c in range(2)],
        axis=1,
    )
    pre_local = jnp.dot(shuffled, encoder, preferred_element_type=F32).astype(BF16)
    pre_act = total(exchange(pre_local.reshape(n_hidden, -1, latents), HIDDEN)) + enc_bias[None, :]
    latent_own = (smooth_scale * jax.nn.softplus(pre_act / smooth_scale)).astype(BF16)
    latent_act = sent_to_all(latent_own, HIDDEN).reshape(tokens, latents)
    recon_local = lax.dot_general(
        decoder, latent_act, (((0,), (1,)), ((), ())), preferred_element_type=F32
    ).astype(BF16)
    recon_pair = both_cores(recon_local).reshape(2, 2, half, tokens)
    recon_mine = total(own(recon_pair, core, 1)).T.astype(BF16).reshape(n_rows_z, -1, half)
    recon = total(exchange(recon_mine, ROWS_Z)) + bias_mine[None, :]
    err_own = (scale * (recon - target)).astype(BF16)
    err_pair = both_cores(sent_to_all(err_own, ROWS_Z).reshape(tokens, half))
    d_err = jnp.concatenate([err_pair[0], err_pair[1]], axis=1)

    back_local = lax.dot_general(
        d_err, decoder, (((1,), (1,)), ((), ())), preferred_element_type=F32
    ).astype(BF16)
    d_latent = total(exchange(back_local.reshape(n_hidden, -1, latents), HIDDEN))
    grad_dec = lax.dot_general(
        latent_act, d_err, (((0,), (0,)), ((), ())), preferred_element_type=F32
    ).astype(BF16)
    d_pre_own = (
        (d_latent + sparsity_weight * scale) * jax.nn.sigmoid(pre_act / smooth_scale)
    ).astype(BF16)
    d_pre = sent_to_all(d_pre_own, HIDDEN).reshape(tokens, latents)
    grad_enc = lax.dot_general(
        shuffled, d_pre, (((0,), (0,)), ((), ())), preferred_element_type=F32
    ).astype(BF16)
    both_recon = both_cores(recon.astype(BF16)).reshape(2, 2, count // 2, half)
    recon_out = own(both_recon, core, 1).transpose(1, 0, 2).reshape(count // 2, width)
    return (recon_out, grad_enc, grad_dec)


def solution(mesh):
    finer = Mesh(
        mesh.devices.reshape(mesh.shape["rows"], 2, 4, 16, 2),
        (R, Y, X, Z, C),
    )
    return jax.shard_map(
        shards,
        mesh=finer,
        in_specs=(
            P(R, HIDDEN_LATENTS),
            P(None, HIDDEN_LATENTS),
            P(None, HIDDEN_LATENTS),
            P(HIDDEN_LATENTS, None),
            P(HIDDEN, ROWS_LATENTS),
            P(ROWS_LATENTS, HIDDEN),
            P(ROWS_LATENTS),
            P(HIDDEN),
            P(),
        ),
        out_specs=(P(ROWS_LATENTS, HIDDEN), P(HIDDEN, ROWS_LATENTS), P(ROWS_LATENTS, HIDDEN)),
        check_vma=False,
    )
```

```python
import math

import jax
import jax.numpy as jnp
from jax import lax
from jax.experimental import pallas as pl
from jax.experimental.pallas import tpu as pltpu
from jax.sharding import Mesh
from jax.sharding import PartitionSpec as P

R, Y, X, Z, C = "rows", "hidden_0", "hidden_1", "latents_0", "latents_1"
HIDDEN = (Y, X)
LATENTS = (Z, C)
HIDDEN_LATENTS = (Y, X, Z, C)
ROWS_LATENTS = (R, Z, C)
ROWS_Z = (R, Z)

smooth_scale = 0.1
sparsity_weight = 0.5
F32 = jnp.float32
BF16 = jnp.bfloat16


def exchange(blocks, axes):
    return lax.all_to_all(blocks, axes, 0, 0, tiled=True)


def copies_of(x, axes):
    return jnp.broadcast_to(x, (lax.axis_size(axes), *x.shape))


def sent_to_all(x, axes):
    return exchange(copies_of(x, axes), axes)


def both_cores(x):
    return lax.all_gather(x, C, axis=0, tiled=False)


def tied(*arrays):
    return lax.optimization_barrier(arrays)


def total(blocks):
    return jnp.sum(blocks.astype(F32), axis=0)


def own(x, index, dim):
    return lax.dynamic_index_in_dim(x, index, dim, keepdims=False)


def gate_kernel(gate_ref, x_ref, gate_act_ref):
    gate_act_ref[...] = jnp.dot(gate_ref[...], x_ref[...], preferred_element_type=F32)


def up_kernel(up_ref, x_ref, gate_act_ref, hidden_ref):
    up_act = jnp.dot(up_ref[...], x_ref[...], preferred_element_type=F32)
    hidden_ref[...] = (jax.nn.gelu(gate_act_ref[...], approximate=True) * up_act).astype(BF16)


def in_vmem(kernel, out_type, weight, x, *rest):
    units, width = weight.shape
    count = x.shape[1]
    whole = pl.BlockSpec(memory_space=pltpu.VMEM)
    return pl.pallas_call(
        kernel,
        in_specs=[whole] * (2 + len(rest)),
        out_specs=whole,
        out_shape=jax.ShapeDtypeStruct((units, count), out_type),
        compiler_params=pltpu.CompilerParams(vmem_limit_bytes=16 * 2**20),
        cost_estimate=pl.CostEstimate(
            flops=2 * units * width * count,
            bytes_accessed=2 * width * (units + count),
            transcendentals=units * count,
        ),
    )(weight, x, *rest)


def gated(gate, up, x):
    return in_vmem(up_kernel, BF16, up, x, in_vmem(gate_kernel, F32, gate, x))


def shards(
    inputs, gate_weight, up_weight, down_weight, encoder, decoder, enc_bias, dec_bias, shuffle_order
):
    tokens = shuffle_order.shape[0]
    n_hidden = lax.axis_size(HIDDEN)
    n_z = lax.axis_size(Z)
    n_rows_z = lax.axis_size(ROWS_Z)
    core = lax.axis_index(C)
    width = decoder.shape[1]
    half = width // 2
    latents = encoder.shape[1]
    units = gate_weight.shape[1]

    few = sent_to_all(inputs.T, Z)
    copies, gate_own, up_own, down_own, order, out_bias = tied(
        copies_of(few, HIDDEN), gate_weight, up_weight, down_weight, shuffle_order, dec_bias
    )
    more = exchange(copies, HIDDEN)
    down_pair = both_cores(down_own).reshape(2 * units, -1)
    count = tokens // n_rows_z
    order_own = lax.dynamic_slice_in_dim(order, lax.axis_index(ROWS_Z) * count, count, 0)
    bias_mine = lax.dynamic_slice_in_dim(out_bias, core * half, half, 0)
    more, gate_own, up_own, down_pair, order_own, bias_mine = tied(
        more, gate_own, up_own, down_pair, order_own, bias_mine
    )
    every = both_cores(more)
    gathered = every.transpose(1, 2, 0, 3, 4).reshape(-1, inputs.shape[0])
    hidden = gated(gate_own.T, up_own.T, gathered)
    hidden_pair = both_cores(hidden).reshape(2 * units, -1)
    mine = lax.dot_general(
        down_pair, hidden_pair, (((0,), (0,)), ((), ())), preferred_element_type=F32
    ).astype(BF16)
    mine = own(mine.reshape(n_hidden, 2, half, -1), core, 1)

    summed = total(exchange(mine, HIDDEN)).T.astype(BF16)
    rows_own = total(exchange(summed.reshape(n_z, -1, half), Z)).astype(BF16)
    mlp_out = both_cores(sent_to_all(rows_own, ROWS_Z).reshape(tokens, half))

    def picked(order):
        return (order[:, None] == jnp.arange(tokens)[None, :]).astype(BF16)

    scale = 1.0 / math.sqrt(tokens)
    target = jnp.dot(picked(order_own), own(mlp_out, core, 0), preferred_element_type=F32)
    mlp_out, target = tied(mlp_out, target)
    pick = picked(shuffle_order)
    shuffled = jnp.concatenate(
        [jnp.dot(pick, mlp_out[c], preferred_element_type=F32).astype(BF16) for c in range(2)],
        axis=1,
    )
    pre_local = jnp.dot(shuffled, encoder, preferred_element_type=F32).astype(BF16)
    pre_act = total(exchange(pre_local.reshape(n_hidden, -1, latents), HIDDEN)) + enc_bias[None, :]
    latent_own = (smooth_scale * jax.nn.softplus(pre_act / smooth_scale)).astype(BF16)
    latent_act = sent_to_all(latent_own, HIDDEN).reshape(tokens, latents)
    recon_local = lax.dot_general(
        decoder, latent_act, (((0,), (1,)), ((), ())), preferred_element_type=F32
    ).astype(BF16)
    recon_pair = both_cores(recon_local).reshape(2, 2, half, tokens)
    recon_mine = total(own(recon_pair, core, 1)).T.astype(BF16).reshape(n_rows_z, -1, half)
    recon = total(exchange(recon_mine, ROWS_Z)) + bias_mine[None, :]
    err_own = (scale * (recon - target)).astype(BF16)
    err_pair = both_cores(sent_to_all(err_own, ROWS_Z).reshape(tokens, half))
    d_err = jnp.concatenate([err_pair[0], err_pair[1]], axis=1)

    back_local = lax.dot_general(
        d_err, decoder, (((1,), (1,)), ((), ())), preferred_element_type=F32
    ).astype(BF16)
    d_latent = total(exchange(back_local.reshape(n_hidden, -1, latents), HIDDEN))
    grad_dec = lax.dot_general(
        latent_act, d_err, (((0,), (0,)), ((), ())), preferred_element_type=F32
    ).astype(BF16)
    d_pre_own = (
        (d_latent + sparsity_weight * scale) * jax.nn.sigmoid(pre_act / smooth_scale)
    ).astype(BF16)
    d_pre = sent_to_all(d_pre_own, HIDDEN).reshape(tokens, latents)
    grad_enc = lax.dot_general(
        shuffled, d_pre, (((0,), (0,)), ((), ())), preferred_element_type=F32
    ).astype(BF16)
    both_recon = both_cores(recon.astype(BF16)).reshape(2, 2, count // 2, half)
    recon_out = own(both_recon, core, 1).transpose(1, 0, 2).reshape(count // 2, width)
    return (recon_out, grad_enc, grad_dec)


def solution(mesh):
    finer = Mesh(
        mesh.devices.reshape(mesh.shape["rows"], 2, 4, 16, 2),
        (R, Y, X, Z, C),
    )
    return jax.shard_map(
        shards,
        mesh=finer,
        in_specs=(
            P(R, HIDDEN_LATENTS),
            P(None, HIDDEN_LATENTS),
            P(None, HIDDEN_LATENTS),
            P(HIDDEN_LATENTS, None),
            P(HIDDEN, ROWS_LATENTS),
            P(ROWS_LATENTS, HIDDEN),
            P(ROWS_LATENTS),
            P(HIDDEN),
            P(),
        ),
        out_specs=(P(ROWS_LATENTS, HIDDEN), P(HIDDEN, ROWS_LATENTS), P(ROWS_LATENTS, HIDDEN)),
        check_vma=False,
    )
```

```python
import math

import jax
import jax.numpy as jnp
from jax import lax
from jax.experimental import pallas as pl
from jax.experimental.pallas import tpu as pltpu
from jax.sharding import Mesh
from jax.sharding import PartitionSpec as P

R, Y, X, Z, C = "rows", "hidden_0", "hidden_1", "latents_0", "latents_1"
HIDDEN = (Y, X)
HIDDEN_X_FIRST = (X, Y)
LATENTS = (Z, C)
HIDDEN_LATENTS = (Y, X, Z, C)
ROWS_LATENTS = (R, Z, C)
ROWS_Z = (R, Z)

smooth_scale = 0.1
sparsity_weight = 0.5
F32 = jnp.float32
BF16 = jnp.bfloat16


def exchange(blocks, axes):
    return lax.all_to_all(blocks, axes, 0, 0, tiled=True)


def copies_of(x, axes):
    return jnp.broadcast_to(x, (lax.axis_size(axes), *x.shape))


def sent_to_all(x, axes):
    return exchange(copies_of(x, axes), axes)


def both_cores(x):
    return lax.all_gather(x, C, axis=0, tiled=False)


def tied(*arrays):
    return lax.optimization_barrier(arrays)


def total(blocks):
    return jnp.sum(blocks.astype(F32), axis=0)


def own(x, index, dim):
    return lax.dynamic_index_in_dim(x, index, dim, keepdims=False)


def gate_kernel(gate_ref, x_ref, gate_act_ref):
    gate_act_ref[...] = jnp.dot(gate_ref[...], x_ref[...], preferred_element_type=F32)


def up_kernel(up_ref, x_ref, gate_act_ref, hidden_ref):
    up_act = jnp.dot(up_ref[...], x_ref[...], preferred_element_type=F32)
    hidden_ref[...] = (jax.nn.gelu(gate_act_ref[...], approximate=True) * up_act).astype(BF16)


def in_vmem(kernel, out_type, weight, x, *rest):
    units, width = weight.shape
    count = x.shape[1]
    whole = pl.BlockSpec(memory_space=pltpu.VMEM)
    return pl.pallas_call(
        kernel,
        in_specs=[whole] * (2 + len(rest)),
        out_specs=whole,
        out_shape=jax.ShapeDtypeStruct((units, count), out_type),
        compiler_params=pltpu.CompilerParams(vmem_limit_bytes=16 * 2**20),
        cost_estimate=pl.CostEstimate(
            flops=2 * units * width * count,
            bytes_accessed=2 * width * (units + count),
            transcendentals=units * count,
        ),
    )(weight, x, *rest)


def gated(gate, up, x):
    return in_vmem(up_kernel, BF16, up, x, in_vmem(gate_kernel, F32, gate, x))


def shards(
    inputs, gate_weight, up_weight, down_weight, encoder, decoder, enc_bias, dec_bias, shuffle_order
):
    tokens = shuffle_order.shape[0]
    n_hidden = lax.axis_size(HIDDEN)
    n_z = lax.axis_size(Z)
    n_rows_z = lax.axis_size(ROWS_Z)
    core = lax.axis_index(C)
    width = decoder.shape[1]
    half = width // 2
    latents = encoder.shape[1]
    units = gate_weight.shape[1]

    few = sent_to_all(inputs.T, Z)
    copies, gate_own, up_own, down_own, order, out_bias = tied(
        copies_of(few, HIDDEN), gate_weight, up_weight, down_weight, shuffle_order, dec_bias
    )
    more = exchange(copies, HIDDEN)
    down_pair = both_cores(down_own).reshape(2 * units, -1)
    count = tokens // n_rows_z
    order_own = lax.dynamic_slice_in_dim(order, lax.axis_index(ROWS_Z) * count, count, 0)
    bias_mine = lax.dynamic_slice_in_dim(out_bias, core * half, half, 0)
    more, gate_own, up_own, down_pair, order_own, bias_mine = tied(
        more, gate_own, up_own, down_pair, order_own, bias_mine
    )
    every = both_cores(more)
    gathered = every.transpose(1, 2, 0, 3, 4).reshape(-1, inputs.shape[0])
    hidden = gated(gate_own.T, up_own.T, gathered)
    hidden_pair = both_cores(hidden).reshape(2 * units, -1)
    mine = lax.dot_general(
        down_pair, hidden_pair, (((0,), (0,)), ((), ())), preferred_element_type=F32
    ).astype(BF16)
    mine = own(mine.reshape(n_hidden, 2, half, -1), core, 1)

    summed = total(exchange(mine, HIDDEN)).T.astype(BF16)
    rows_own = total(exchange(summed.reshape(n_z, -1, half), Z)).astype(BF16)
    mlp_out = both_cores(sent_to_all(rows_own, ROWS_Z).reshape(tokens, half))

    def picked(order):
        return (order[:, None] == jnp.arange(tokens)[None, :]).astype(BF16)

    scale = 1.0 / math.sqrt(tokens)
    target = jnp.dot(picked(order_own), own(mlp_out, core, 0), preferred_element_type=F32)
    mlp_out, target = tied(mlp_out, target)
    pick = picked(shuffle_order)
    shuffled = jnp.concatenate(
        [jnp.dot(pick, mlp_out[c], preferred_element_type=F32).astype(BF16) for c in range(2)],
        axis=1,
    )
    pre_local = jnp.dot(shuffled, encoder, preferred_element_type=F32).astype(BF16)
    pre_act = total(exchange(pre_local.reshape(n_hidden, -1, latents), HIDDEN_X_FIRST)) + enc_bias[None, :]
    latent_own = (smooth_scale * jax.nn.softplus(pre_act / smooth_scale)).astype(BF16)
    latent_act = sent_to_all(latent_own, HIDDEN_X_FIRST).reshape(tokens, latents)
    recon_local = lax.dot_general(
        decoder, latent_act, (((0,), (1,)), ((), ())), preferred_element_type=F32
    ).astype(BF16)
    recon_pair = both_cores(recon_local).reshape(2, 2, half, tokens)
    recon_mine = total(own(recon_pair, core, 1)).T.astype(BF16).reshape(n_rows_z, -1, half)
    recon = total(exchange(recon_mine, ROWS_Z)) + bias_mine[None, :]
    err_own = (scale * (recon - target)).astype(BF16)
    err_pair = both_cores(sent_to_all(err_own, ROWS_Z).reshape(tokens, half))
    d_err = jnp.concatenate([err_pair[0], err_pair[1]], axis=1)

    back_local = lax.dot_general(
        d_err, decoder, (((1,), (1,)), ((), ())), preferred_element_type=F32
    ).astype(BF16)
    d_latent = total(exchange(back_local.reshape(n_hidden, -1, latents), HIDDEN_X_FIRST))
    grad_dec = lax.dot_general(
        latent_act, d_err, (((0,), (0,)), ((), ())), preferred_element_type=F32
    ).astype(BF16)
    d_pre_own = (
        (d_latent + sparsity_weight * scale) * jax.nn.sigmoid(pre_act / smooth_scale)
    ).astype(BF16)
    d_pre = sent_to_all(d_pre_own, HIDDEN_X_FIRST).reshape(tokens, latents)
    grad_enc = lax.dot_general(
        shuffled, d_pre, (((0,), (0,)), ((), ())), preferred_element_type=F32
    ).astype(BF16)
    both_recon = both_cores(recon.astype(BF16)).reshape(2, 2, count // 2, half)
    recon_out = own(both_recon, core, 1).transpose(1, 0, 2).reshape(count // 2, width)
    return (recon_out, grad_enc, grad_dec)


def solution(mesh):
    finer = Mesh(
        mesh.devices.reshape(mesh.shape["rows"], 2, 4, 16, 2),
        (R, Y, X, Z, C),
    )
    return jax.shard_map(
        shards,
        mesh=finer,
        in_specs=(
            P(R, HIDDEN_LATENTS),
            P(None, HIDDEN_LATENTS),
            P(None, HIDDEN_LATENTS),
            P(HIDDEN_LATENTS, None),
            P(HIDDEN, ROWS_LATENTS),
            P(ROWS_LATENTS, HIDDEN),
            P(ROWS_LATENTS),
            P(HIDDEN),
            P(),
        ),
        out_specs=(P(ROWS_LATENTS, HIDDEN), P(HIDDEN, ROWS_LATENTS), P(ROWS_LATENTS, HIDDEN)),
        check_vma=False,
    )
```

```python
import math

import jax
import jax.numpy as jnp
from jax import lax
from jax.experimental import pallas as pl
from jax.experimental.pallas import tpu as pltpu
from jax.sharding import Mesh
from jax.sharding import PartitionSpec as P

R, Y, X, C = "rows", "hidden_0", "hidden_1", "core"
Z_FAR, Z_NEAR = "latents_0", "latents_1"
Z = (Z_FAR, Z_NEAR)
HIDDEN = (Y, X)
HIDDEN_X_FIRST = (X, Y)
LATENTS = (Z_FAR, Z_NEAR, C)
HIDDEN_LATENTS = HIDDEN + LATENTS
ROWS_LATENTS = (R,) + LATENTS
ROWS_Z = (R,) + Z
NEAR_FIRST = (Z_NEAR, R, Z_FAR)

smooth_scale = 0.1
sparsity_weight = 0.5
F32 = jnp.float32
BF16 = jnp.bfloat16


def exchange(blocks, axes):
    return lax.all_to_all(blocks, axes, 0, 0, tiled=True)


def copies_of(x, axes):
    return jnp.broadcast_to(x, (lax.axis_size(axes), *x.shape))


def sent_to_all(x, axes):
    return exchange(copies_of(x, axes), axes)


def both_cores(x):
    return lax.all_gather(x, C, axis=0, tiled=False)


def tied(*arrays):
    return lax.optimization_barrier(arrays)


def near_first(x, count):
    far, near = lax.axis_size(Z_FAR), lax.axis_size(Z_NEAR)
    return x.reshape(-1, far, near, count).transpose(2, 0, 1, 3).reshape(-1)


def total(blocks):
    return jnp.sum(blocks.astype(F32), axis=0)


def own(x, index, dim):
    return lax.dynamic_index_in_dim(x, index, dim, keepdims=False)


def gate_kernel(gate_ref, x_ref, gate_act_ref):
    gate_act_ref[...] = jnp.dot(gate_ref[...], x_ref[...], preferred_element_type=F32)


def up_kernel(up_ref, x_ref, gate_act_ref, hidden_ref):
    up_act = jnp.dot(up_ref[...], x_ref[...], preferred_element_type=F32)
    hidden_ref[...] = (jax.nn.gelu(gate_act_ref[...], approximate=True) * up_act).astype(BF16)


def in_vmem(kernel, out_type, weight, x, *rest):
    units, width = weight.shape
    count = x.shape[1]
    whole = pl.BlockSpec(memory_space=pltpu.VMEM)
    return pl.pallas_call(
        kernel,
        in_specs=[whole] * (2 + len(rest)),
        out_specs=whole,
        out_shape=jax.ShapeDtypeStruct((units, count), out_type),
        compiler_params=pltpu.CompilerParams(vmem_limit_bytes=16 * 2**20),
        cost_estimate=pl.CostEstimate(
            flops=2 * units * width * count,
            bytes_accessed=2 * width * (units + count),
            transcendentals=units * count,
        ),
    )(weight, x, *rest)


def gated(gate, up, x):
    return in_vmem(up_kernel, BF16, up, x, in_vmem(gate_kernel, F32, gate, x))


def shards(
    inputs, gate_weight, up_weight, down_weight, encoder, decoder, enc_bias, dec_bias, shuffle_order
):
    tokens = shuffle_order.shape[0]
    n_hidden = lax.axis_size(HIDDEN)
    n_z = lax.axis_size(Z)
    n_rows_z = lax.axis_size(ROWS_Z)
    core = lax.axis_index(C)
    width = decoder.shape[1]
    half = width // 2
    latents = encoder.shape[1]
    units = gate_weight.shape[1]

    few = sent_to_all(inputs.T, Z)
    copies, gate_own, up_own, down_own, order, out_bias = tied(
        copies_of(few, HIDDEN_X_FIRST), gate_weight, up_weight, down_weight, shuffle_order, dec_bias
    )
    more = exchange(copies, HIDDEN_X_FIRST)
    down_pair = both_cores(down_own).reshape(2 * units, -1)
    count = tokens // n_rows_z
    order_own = lax.dynamic_slice_in_dim(order, lax.axis_index(ROWS_Z) * count, count, 0)
    order = near_first(order, count)
    bias_mine = lax.dynamic_slice_in_dim(out_bias, core * half, half, 0)
    more, gate_own, up_own, down_pair, order, order_own, bias_mine = tied(
        more, gate_own, up_own, down_pair, order, order_own, bias_mine
    )
    every = both_cores(more)
    n_x = lax.axis_size(X)
    blocks = every.reshape(2, n_x, n_hidden // n_x, *every.shape[2:])
    gathered = blocks.transpose(2, 1, 3, 0, 4, 5).reshape(-1, inputs.shape[0])
    hidden = gated(gate_own.T, up_own.T, gathered)
    hidden_pair = both_cores(hidden).reshape(2 * units, -1)
    mine = lax.dot_general(
        down_pair, hidden_pair, (((0,), (0,)), ((), ())), preferred_element_type=F32
    ).astype(BF16)
    mine = own(mine.reshape(-1, n_x, 2, half, inputs.shape[0]), core, 2)
    mine = mine.transpose(1, 0, 2, 3).reshape(n_hidden, half, -1)

    summed = total(exchange(mine, HIDDEN_X_FIRST)).T.astype(BF16)
    rows_own = total(exchange(summed.reshape(n_z, -1, half), Z)).astype(BF16)
    mlp_out = both_cores(sent_to_all(rows_own, NEAR_FIRST).reshape(tokens, half))

    held = near_first(jnp.arange(tokens), count)

    def picked(order):
        return (order[:, None] == held[None, :]).astype(BF16)

    scale = 1.0 / math.sqrt(tokens)
    target = jnp.dot(picked(order_own), own(mlp_out, core, 0), preferred_element_type=F32)
    mlp_out, target = tied(mlp_out, target)
    pick = picked(order)
    shuffled = jnp.concatenate(
        [jnp.dot(pick, mlp_out[c], preferred_element_type=F32).astype(BF16) for c in range(2)],
        axis=1,
    )
    pre_local = jnp.dot(shuffled, encoder, preferred_element_type=F32).astype(BF16)
    pre_act = total(exchange(pre_local.reshape(n_hidden, -1, latents), HIDDEN_X_FIRST)) + enc_bias[None, :]
    latent_own = (smooth_scale * jax.nn.softplus(pre_act / smooth_scale)).astype(BF16)
    latent_act = sent_to_all(latent_own, HIDDEN_X_FIRST).reshape(tokens, latents)
    recon_local = lax.dot_general(
        decoder, latent_act, (((0,), (1,)), ((), ())), preferred_element_type=F32
    ).astype(BF16)
    recon_pair = both_cores(recon_local).reshape(2, 2, half, tokens)
    recon_mine = total(own(recon_pair, core, 1)).T.astype(BF16).reshape(n_rows_z, -1, half)
    recon = total(exchange(recon_mine, NEAR_FIRST)) + bias_mine[None, :]
    err_own = (scale * (recon - target)).astype(BF16)
    err_pair = both_cores(sent_to_all(err_own, NEAR_FIRST).reshape(tokens, half))
    d_err = jnp.concatenate([err_pair[0], err_pair[1]], axis=1)

    back_local = lax.dot_general(
        d_err, decoder, (((1,), (1,)), ((), ())), preferred_element_type=F32
    ).astype(BF16)
    d_latent = total(exchange(back_local.reshape(n_hidden, -1, latents), HIDDEN_X_FIRST))
    grad_dec = lax.dot_general(
        latent_act, d_err, (((0,), (0,)), ((), ())), preferred_element_type=F32
    ).astype(BF16)
    d_pre_own = (
        (d_latent + sparsity_weight * scale) * jax.nn.sigmoid(pre_act / smooth_scale)
    ).astype(BF16)
    d_pre = sent_to_all(d_pre_own, HIDDEN_X_FIRST).reshape(tokens, latents)
    grad_enc = lax.dot_general(
        shuffled, d_pre, (((0,), (0,)), ((), ())), preferred_element_type=F32
    ).astype(BF16)
    both_recon = both_cores(recon.astype(BF16)).reshape(2, 2, count // 2, half)
    recon_out = own(both_recon, core, 1).transpose(1, 0, 2).reshape(count // 2, width)
    return (recon_out, grad_enc, grad_dec)


def solution(mesh):
    finer = Mesh(
        mesh.devices.reshape(mesh.shape["rows"], 2, 4, 8, 2, 2),
        (R, Y, X, Z_FAR, Z_NEAR, C),
    )
    return jax.shard_map(
        shards,
        mesh=finer,
        in_specs=(
            P(R, HIDDEN_LATENTS),
            P(None, HIDDEN_LATENTS),
            P(None, HIDDEN_LATENTS),
            P(HIDDEN_LATENTS, None),
            P(HIDDEN, ROWS_LATENTS),
            P(ROWS_LATENTS, HIDDEN),
            P(ROWS_LATENTS),
            P(HIDDEN),
            P(),
        ),
        out_specs=(P(ROWS_LATENTS, HIDDEN), P(HIDDEN, ROWS_LATENTS), P(ROWS_LATENTS, HIDDEN)),
        check_vma=False,
    )
```

```python
import math

import jax
import jax.numpy as jnp
from jax import lax
from jax.experimental import pallas as pl
from jax.experimental.pallas import tpu as pltpu
from jax.sharding import Mesh
from jax.sharding import PartitionSpec as P

R, Y, X, C = "rows", "hidden_0", "hidden_1", "core"
Z_FAR, Z_NEAR = "latents_0", "latents_1"
Z = (Z_FAR, Z_NEAR)
Z_NEAR_FIRST = (Z_NEAR, Z_FAR)
HIDDEN = (Y, X)
HIDDEN_X_FIRST = (X, Y)
LATENTS = (Z_FAR, Z_NEAR, C)
HIDDEN_LATENTS = HIDDEN + LATENTS
ROWS_LATENTS = (R,) + LATENTS
ROWS_Z = (R,) + Z
NEAR_FIRST = (Z_NEAR, R, Z_FAR)

smooth_scale = 0.1
sparsity_weight = 0.5
F32 = jnp.float32
BF16 = jnp.bfloat16


def exchange(blocks, axes):
    return lax.all_to_all(blocks, axes, 0, 0, tiled=True)


def copies_of(x, axes):
    return jnp.broadcast_to(x, (lax.axis_size(axes), *x.shape))


def sent_to_all(x, axes):
    return exchange(copies_of(x, axes), axes)


def both_cores(x):
    return lax.all_gather(x, C, axis=0, tiled=False)


def tied(*arrays):
    return lax.optimization_barrier(arrays)


def near_first(x, count):
    far, near = lax.axis_size(Z_FAR), lax.axis_size(Z_NEAR)
    return x.reshape(-1, far, near, count).transpose(2, 0, 1, 3).reshape(-1)


def total(blocks):
    return jnp.sum(blocks.astype(F32), axis=0)


def own(x, index, dim):
    return lax.dynamic_index_in_dim(x, index, dim, keepdims=False)


def gate_kernel(gate_ref, x_ref, gate_act_ref):
    gate_act_ref[...] = jnp.dot(gate_ref[...], x_ref[...], preferred_element_type=F32)


def up_kernel(up_ref, x_ref, gate_act_ref, hidden_ref):
    up_act = jnp.dot(up_ref[...], x_ref[...], preferred_element_type=F32)
    hidden_ref[...] = (jax.nn.gelu(gate_act_ref[...], approximate=True) * up_act).astype(BF16)


def in_vmem(kernel, out_type, weight, x, *rest):
    units, width = weight.shape
    count = x.shape[1]
    whole = pl.BlockSpec(memory_space=pltpu.VMEM)
    return pl.pallas_call(
        kernel,
        in_specs=[whole] * (2 + len(rest)),
        out_specs=whole,
        out_shape=jax.ShapeDtypeStruct((units, count), out_type),
        compiler_params=pltpu.CompilerParams(vmem_limit_bytes=16 * 2**20),
        cost_estimate=pl.CostEstimate(
            flops=2 * units * width * count,
            bytes_accessed=2 * width * (units + count),
            transcendentals=units * count,
        ),
    )(weight, x, *rest)


def gated(gate, up, x):
    return in_vmem(up_kernel, BF16, up, x, in_vmem(gate_kernel, F32, gate, x))


def shards(
    inputs, gate_weight, up_weight, down_weight, encoder, decoder, enc_bias, dec_bias, shuffle_order
):
    tokens = shuffle_order.shape[0]
    n_hidden = lax.axis_size(HIDDEN)
    n_z = lax.axis_size(Z)
    n_far = lax.axis_size(Z_FAR)
    n_rows_z = lax.axis_size(ROWS_Z)
    core = lax.axis_index(C)
    width = decoder.shape[1]
    half = width // 2
    latents = encoder.shape[1]
    units = gate_weight.shape[1]

    few = sent_to_all(inputs.T, Z_NEAR_FIRST)
    few = few.reshape(-1, n_far, *few.shape[1:]).swapaxes(0, 1).reshape(few.shape)
    copies, gate_own, up_own, down_own, order, out_bias = tied(
        copies_of(few, HIDDEN_X_FIRST), gate_weight, up_weight, down_weight, shuffle_order, dec_bias
    )
    more = exchange(copies, HIDDEN_X_FIRST)
    down_pair = both_cores(down_own).reshape(2 * units, -1)
    count = tokens // n_rows_z
    order_own = lax.dynamic_slice_in_dim(order, lax.axis_index(ROWS_Z) * count, count, 0)
    order = near_first(order, count)
    bias_mine = lax.dynamic_slice_in_dim(out_bias, core * half, half, 0)
    more, gate_own, up_own, down_pair, order, order_own, bias_mine = tied(
        more, gate_own, up_own, down_pair, order, order_own, bias_mine
    )
    every = both_cores(more)
    n_x = lax.axis_size(X)
    blocks = every.reshape(2, n_x, n_hidden // n_x, *every.shape[2:])
    gathered = blocks.transpose(2, 1, 3, 0, 4, 5).reshape(-1, inputs.shape[0])
    hidden = gated(gate_own.T, up_own.T, gathered)
    hidden_pair = both_cores(hidden).reshape(2 * units, -1)
    mine = lax.dot_general(
        down_pair, hidden_pair, (((0,), (0,)), ((), ())), preferred_element_type=F32
    ).astype(BF16)
    mine = own(mine.reshape(-1, n_x, 2, half, inputs.shape[0]), core, 2)
    mine = mine.transpose(1, 0, 2, 3).reshape(n_hidden, half, -1)

    summed = total(exchange(mine, HIDDEN_X_FIRST)).T.astype(BF16)
    rows_own = total(exchange(summed.reshape(n_z, -1, half), Z_NEAR_FIRST)).astype(BF16)
    mlp_out = both_cores(sent_to_all(rows_own, NEAR_FIRST).reshape(tokens, half))

    held = jnp.arange(tokens).reshape(2, -1, n_far * count).swapaxes(0, 1).reshape(-1)

    def picked(order):
        return (order[:, None] == held[None, :]).astype(BF16)

    scale = 1.0 / math.sqrt(tokens)
    target = jnp.dot(picked(order_own), own(mlp_out, core, 0), preferred_element_type=F32)
    mlp_out, target = tied(mlp_out, target)
    pick = picked(order)
    shuffled = jnp.concatenate(
        [jnp.dot(pick, mlp_out[c], preferred_element_type=F32).astype(BF16) for c in range(2)],
        axis=1,
    )
    pre_local = jnp.dot(shuffled, encoder, preferred_element_type=F32).astype(BF16)
    pre_act = total(exchange(pre_local.reshape(n_hidden, -1, latents), HIDDEN_X_FIRST)) + enc_bias[None, :]
    latent_own = (smooth_scale * jax.nn.softplus(pre_act / smooth_scale)).astype(BF16)
    latent_act = sent_to_all(latent_own, HIDDEN_X_FIRST).reshape(tokens, latents)
    recon_local = lax.dot_general(
        decoder, latent_act, (((0,), (1,)), ((), ())), preferred_element_type=F32
    ).astype(BF16)
    recon_pair = both_cores(recon_local).reshape(2, 2, half, tokens)
    recon_mine = total(own(recon_pair, core, 1)).T.astype(BF16).reshape(n_rows_z, -1, half)
    recon = total(exchange(recon_mine, NEAR_FIRST)) + bias_mine[None, :]
    err_own = (scale * (recon - target)).astype(BF16)
    err_pair = both_cores(sent_to_all(err_own, NEAR_FIRST).reshape(tokens, half))
    d_err = jnp.concatenate([err_pair[0], err_pair[1]], axis=1)

    back_local = lax.dot_general(
        d_err, decoder, (((1,), (1,)), ((), ())), preferred_element_type=F32
    ).astype(BF16)
    d_latent = total(exchange(back_local.reshape(n_hidden, -1, latents), HIDDEN_X_FIRST))
    grad_dec = lax.dot_general(
        latent_act, d_err, (((0,), (0,)), ((), ())), preferred_element_type=F32
    ).astype(BF16)
    d_pre_own = (
        (d_latent + sparsity_weight * scale) * jax.nn.sigmoid(pre_act / smooth_scale)
    ).astype(BF16)
    d_pre = sent_to_all(d_pre_own, HIDDEN_X_FIRST).reshape(tokens, latents)
    grad_enc = lax.dot_general(
        shuffled, d_pre, (((0,), (0,)), ((), ())), preferred_element_type=F32
    ).astype(BF16)
    both_recon = both_cores(recon.astype(BF16)).reshape(2, 2, count // 2, half)
    recon_out = own(both_recon, core, 1).transpose(1, 0, 2).reshape(count // 2, width)
    return (recon_out, grad_enc, grad_dec)


def solution(mesh):
    finer = Mesh(
        mesh.devices.reshape(mesh.shape["rows"], 2, 4, 8, 2, 2),
        (R, Y, X, Z_FAR, Z_NEAR, C),
    )
    return jax.shard_map(
        shards,
        mesh=finer,
        in_specs=(
            P(R, HIDDEN_LATENTS),
            P(None, HIDDEN_LATENTS),
            P(None, HIDDEN_LATENTS),
            P(HIDDEN_LATENTS, None),
            P(HIDDEN, ROWS_LATENTS),
            P(ROWS_LATENTS, HIDDEN),
            P(ROWS_LATENTS),
            P(HIDDEN),
            P(),
        ),
        out_specs=(P(ROWS_LATENTS, HIDDEN), P(HIDDEN, ROWS_LATENTS), P(ROWS_LATENTS, HIDDEN)),
        check_vma=False,
    )
```
